1024 devices in a mesh: dp: 16 (over y, core), mp: 64 (over z, x).
Axes of the slice: x: 4, y: 8, z: 16, core: 2. Of those that a mesh axis runs over, the one named last changes fastest.
Arguments:
- qkv: bfloat16 [131072, 3840], P(('dp', 'mp')), may hold values from -16 to 16
- send_pos: int32 [16384], P(('dp', 'mp')), may hold values from 0 to 15, as said below
- recv_pos: int32 [16384], P(('dp', 'mp')), may hold values from 0 to 15, as said below
- block_image: int32 [16384], P(('dp', 'mp')), may hold values from 0 to 15, as said below
- owner: int32 [131072, 1], P(('dp', 'mp')), may hold values from 0 to 63; in each aligned block of 128 rows (0 to 127, 128 to 255, ...) at most 3 rows name the same one
- cotangent: bfloat16 [131072, 640], P(('dp', 'mp')), may hold values from -0.109375 to 0.109375
- out_weight: bfloat16 [1280, 1280], replicated, may hold values from -0.15625 to 0.15625
Outputs:
- attended_sent: bfloat16 [196608, 1280], P(('dp', 'mp'))
- grad_out_weight: float32 [409600], P(('dp', 'mp'))
The draws below stay inside these ranges and needn't reach their ends.
Inputs may be any that keep to these rules, and one draw needn't show every extreme that they name: `send_pos`: within a device the 16 values are distinct; value p + c sends the block to dp index p of the same mp index, slot c. Every device sends exactly 1 block to each of 16 distinct dp indices. `recv_pos`: within a device the 16 values are distinct; value q + c takes the block that dp index q of the same mp index sent in slot c to this device, and that block exists. Every device receives exactly 1 block from each of 16 distinct dp indices. `block_image`: never falls along a device's working blocks and starts at 0 on each device; an image is 1 to 16 blocks; some device holds one image of 16 blocks, and some device holds 16 images of one block each. Of one device's rows, at most 3 have the same owner, and some device has exactly 3 rows for some owner.
All inputs are finite; a program needn't handle non-finite values.
Results may differ from the reference program's by a relative error of at most 0.0057.
Values may be sent and summed in bfloat16 or wider, within the bound.
A program may use at most 32 MiB of HBM per device.

```python
import math
import jax
import jax.numpy as jnp
import numpy as np
from jax import lax

D = 1280
HEADS = 16
HEAD_DIM = 80
GW = 640
BR = 8
NBW = 16
CAP = 1
ROWS = 128
MOST_R = 3
TOTAL_ROWS = 131072
N_DP = 16
N_MP = 64


def draw_qkv(key, part):
    shape = (TOTAL_ROWS, 3, HEADS, HEAD_DIM)
    base = jax.random.truncated_normal(jax.random.fold_in(key, 101), -4.0, 4.0, shape, jnp.float32)
    spread = jnp.exp(jax.random.uniform(jax.random.fold_in(key, 102), (TOTAL_ROWS, 1, HEADS, 1), jnp.float32, math.log(0.4), math.log(4.0)))
    is_query = jnp.arange(3)[None, :, None, None] == 0
    values = jnp.where(is_query, base * spread, base)
    return values.reshape(TOTAL_ROWS, 3 * D).astype(jnp.bfloat16)


def order_table(key):
    scores = jax.random.randint(key, (N_DP, N_MP, NBW), 0, 1 << 20) * NBW + jnp.arange(NBW, dtype=jnp.int32)
    return jnp.argsort(scores, axis=-1).astype(jnp.int32)


def plan_tables(key):
    groups = NBW // CAP
    base = jax.random.fold_in(key, 21)

    def column_shifts(index):
        return jax.random.permutation(jax.random.fold_in(base, index), N_DP)[:groups].astype(jnp.int32)
    shifts = jax.vmap(column_shifts)(jnp.arange(N_MP, dtype=jnp.int32))
    shift_grid = jnp.broadcast_to(shifts[None, :, :], (N_DP, N_MP, groups))
    dp_grid = jnp.arange(N_DP, dtype=jnp.int32)[:, None, None]
    send_edge = order_table(jax.random.fold_in(key, 22))
    send_shift = jnp.take_along_axis(shift_grid, send_edge // CAP, axis=2)
    send_table = (dp_grid + send_shift) % N_DP * CAP + send_edge % CAP
    recv_edge = order_table(jax.random.fold_in(key, 23))
    recv_shift = jnp.take_along_axis(shift_grid, recv_edge // CAP, axis=2)
    recv_table = (dp_grid - recv_shift) % N_DP * CAP + recv_edge % CAP
    return (send_table.reshape(-1).astype(jnp.int32), recv_table.reshape(-1).astype(jnp.int32))


def draw_send_pos(key, part):
    return plan_tables(key)[0]


def draw_recv_pos(key, part):
    return plan_tables(key)[1]


def draw_block_image(key, part):
    cuts = jax.random.randint(jax.random.fold_in(key, 31), (N_DP, N_MP, NBW), 0, 3) == 0
    first = jnp.arange(NBW)[None, None, :] == 0
    single = (jnp.arange(N_DP)[:, None, None] == 0) & (jnp.arange(N_MP)[None, :, None] == 0)
    every = (jnp.arange(N_DP)[:, None, None] == 1) & (jnp.arange(N_MP)[None, :, None] == 0)
    cuts = cuts | every
    cuts = cuts & jnp.logical_not(first) & jnp.logical_not(single)
    return jnp.cumsum(cuts.astype(jnp.int32), axis=-1).reshape(-1).astype(jnp.int32)


def level_of(rng, shape, cuts, least, largest):
    loudness, own = 1.0, jax.random.fold_in(rng, 6)
    for dim, blocks in cuts:
        draws = jnp.exp(jax.random.uniform(jax.random.fold_in(own, dim), (blocks,), jnp.float32, least / len(cuts), largest / len(cuts)))
        loudness = loudness * jnp.repeat(draws, shape[dim] // blocks).reshape([-1 if axis == dim else 1 for axis in range(len(shape))])
    return loudness


def assign_block(own_key, own, number, rows, count, top, bound, lean):
    ranking = jax.random.permutation(own_key, count)
    heavy_load, common = load_shares(count, rows * top, bound, lean, True), load_shares(count, rows * top, bound, lean, False)
    places = jnp.arange(count)

    def named(lengths, offset_by):
        used = int((lengths > 0).sum())
        fixed = max(1, used // 4)
        shifted = fixed + (places - fixed + offset_by * (used - fixed)) % max(1, count - fixed)
        return jnp.zeros((count,), jnp.int32).at[ranking[jnp.where(places < fixed, places, shifted)]].set(jnp.asarray(lengths, jnp.int32))

    lengths = jnp.where(number % 4 == 0, named(heavy_load, number // 4), named(common, number - number // 4 - 1))
    mixed = jax.random.permutation(jax.random.fold_in(own, 3), count)
    donor, taker = mixed[0:count // 2 * 2:2], mixed[1:count // 2 * 2:2]
    margin = jnp.minimum(lengths[donor] - 1, bound - lengths[taker]) // 2
    margin = jnp.where((donor == ranking[0]) | (taker == ranking[0]) | (lengths[taker] == 0), 0, jnp.maximum(margin, 0))
    shifted = jax.random.randint(jax.random.fold_in(own, 4), (count // 2,), 0, 1 << 20) % (margin + 1)
    lengths = lengths.at[donor].add(-shifted).at[taker].add(shifted)
    items = jnp.searchsorted(jnp.cumsum(lengths), jnp.arange(rows * top), side="right").astype(jnp.int32)
    table = items.reshape(top, rows).T
    table = table[jax.random.permutation(jax.random.fold_in(own, 1), rows)]
    offset_by = jax.random.randint(jax.random.fold_in(own, 2), (rows, 1), 0, top)
    return jnp.take_along_axis(table, (jnp.arange(top)[None, :] + offset_by) % top, axis=1)


def load_shares(amount, total, most, lean, full):
    portions = [(1 << 20) // math.isqrt(standing ** lean) + 1 for standing in range(1, amount + 1)]
    largest = most if full else min(most, max(-(-total // amount), total * portions[0] // sum(portions)))
    least = 1 if total - largest >= amount - 1 else 0
    given, spare = [largest] + [least] * (amount - 1), total - largest - least * (amount - 1)
    while spare > 0:
        free = [i for i in range(1, amount) if given[i] < largest] or [i for i in range(1, amount) if given[i] < most]
        mass, budget = sum([portions[i] for i in free]), spare
        for i in free:
            extra = min(most - given[i], max(1, budget * portions[i] // mass), spare)
            given[i] = given[i] + extra
            spare = spare - extra
    return np.array(given)


def bell_draw(stream_key, dims, deviation, bound, pieces=(), held_as=jnp.bfloat16):
    array = deviation * jax.random.normal(stream_key, dims, jnp.float32)
    if pieces:
        array = array * level_of(stream_key, dims, pieces, -0.22, 0.18)
    return jnp.clip(array, -bound, bound).astype(held_as)


def setup_inputs(seed: int = 0) -> dict:
    seeds = jax.random.split(jax.random.key(seed), 8)
    qkv = draw_qkv(jax.random.fold_in(seeds[7], 71), 0)
    send_pos = draw_send_pos(jax.random.fold_in(seeds[7], 71), 0)
    recv_pos = draw_recv_pos(jax.random.fold_in(seeds[7], 71), 0)
    block_image = draw_block_image(jax.random.fold_in(seeds[7], 71), 0)
    owner_keys = jax.random.split(jax.random.fold_in(seeds[4], 1), TOTAL_ROWS // ROWS)
    owner_turns = jax.random.permutation(jax.random.fold_in(seeds[4], 3), TOTAL_ROWS // ROWS)
    owner = jax.vmap(lambda own, number: assign_block(jax.random.fold_in(seeds[4], 2), own, number, ROWS, N_MP, 1, MOST_R, 1))(owner_keys, owner_turns).reshape((TOTAL_ROWS, 1))
    cotangent = bell_draw(seeds[5], (TOTAL_ROWS, GW), 0.007, 0.109375, ((0, 1024),))
    out_weight = bell_draw(seeds[6], (D, D), D ** -0.5, 0.15625)
    return dict(qkv=qkv, send_pos=send_pos, recv_pos=recv_pos, block_image=block_image, owner=owner, cotangent=cotangent, out_weight=out_weight)


def attend(packed, images):
    count = packed.shape[0]
    whole = packed.astype(jnp.float32).reshape(count, 3, HEADS, HEAD_DIM)
    query = whole[:, 0]
    keys = whole[:, 1]
    values = whole[:, 2]
    scores = jnp.einsum('qhd,khd->hqk', query, keys) / math.sqrt(HEAD_DIM)
    row_image = jnp.repeat(images, BR)
    allowed = (row_image[:, None] == row_image[None, :])[None]
    masked = jnp.where(allowed, scores, -jnp.inf)
    highest = lax.optimization_barrier(jnp.max(masked, axis=-1, keepdims=True))
    weights = jnp.where(allowed, jnp.exp(masked - highest), 0.0)
    probs = (weights / lax.optimization_barrier(jnp.sum(weights, axis=-1, keepdims=True))).astype(jnp.bfloat16)
    context = jnp.einsum('hqk,khd->qhd', probs.astype(jnp.float32), values)
    return context.reshape(count, D).astype(jnp.bfloat16)

def attend_column(inputs):
    return jax.vmap(attend)(inputs[0], inputs[1])

def reference(qkv, send_pos, recv_pos, block_image, owner, cotangent, out_weight):
    width = 3 * D
    blocks = qkv.reshape(N_DP, N_MP, NBW, BR, width)
    sender = send_pos.reshape(N_DP, N_MP, NBW)
    taker = recv_pos.reshape(N_DP, N_MP, NBW)
    dp_grid = jnp.broadcast_to(jnp.arange(N_DP, dtype=jnp.int32)[:, None, None], (N_DP, N_MP, NBW))
    mp_grid = jnp.broadcast_to(jnp.arange(N_MP, dtype=jnp.int32)[None, :, None], (N_DP, N_MP, NBW))
    slot_grid = jnp.broadcast_to(jnp.arange(NBW, dtype=jnp.int32)[None, None, :], (N_DP, N_MP, NBW))
    table = jnp.zeros((N_DP, N_MP, N_DP * CAP), jnp.int32).at[dp_grid, mp_grid, sender].set(slot_grid)
    source_dp = (taker // CAP).astype(jnp.int32)
    source_slot = table[source_dp, mp_grid, (dp_grid * CAP + taker % CAP).astype(jnp.int32)]
    packed = blocks[source_dp, mp_grid, source_slot].reshape(N_DP, N_MP, ROWS, width)
    images = block_image.reshape(N_DP, N_MP, NBW)
    context = lax.map(attend_column, (packed, images))
    flat_context = context.reshape(TOTAL_ROWS, D)
    attended = jnp.dot(flat_context, out_weight, preferred_element_type=jnp.float32).astype(jnp.bfloat16)
    target = owner.reshape(N_DP, N_MP, ROWS)
    member = (target[..., None] == jnp.arange(N_MP, dtype=jnp.int32)).astype(jnp.int32)
    before = jnp.cumsum(member, axis=2) - member
    rank = lax.optimization_barrier(jnp.sum(before * member, axis=3)).astype(jnp.int32)
    row_dp = jnp.broadcast_to(jnp.arange(N_DP, dtype=jnp.int32)[:, None, None], (N_DP, N_MP, ROWS))
    row_mp = jnp.broadcast_to(jnp.arange(N_MP, dtype=jnp.int32)[None, :, None], (N_DP, N_MP, ROWS))
    sent = jnp.zeros((N_DP, N_MP, N_MP, MOST_R, D), jnp.bfloat16)
    sent = sent.at[row_dp, target, row_mp, rank].set(attended.reshape(N_DP, N_MP, ROWS, D))
    attended_sent = sent.reshape(N_DP * N_MP * N_MP * MOST_R, D)
    grad_matrix = jnp.dot(flat_context[:, :GW].T, cotangent, preferred_element_type=jnp.float32)
    return (attended_sent, grad_matrix.reshape(GW * GW))
```

```python
import functools
import math

import jax
import jax.numpy as jnp
from jax import lax
from jax.experimental import pallas as pl
from jax.experimental.pallas import tpu as pltpu
from jax.sharding import PartitionSpec as P

MESH = pl.DeviceIdType.MESH
D = 1280
HEAD = 80
GW = 640
BR = 8
NX = 4
CHUNKS = 4
HPC = 4
CC = HPC * HEAD
TILES = ((0, 1, 2), (3, 4), (5, 6, 7), (8, 9))
WIDTHS = tuple(3 * 128 * len(t) for t in TILES)
STARTS = tuple(sum(WIDTHS[:c]) for c in range(CHUNKS))
AROWS = 128
PIECE = 400
PADDED = 512
F32 = jnp.float32
BF16 = jnp.bfloat16


def place_of(kind, tile):
    for c, tiles in enumerate(TILES):
        if tile in tiles:
            return STARTS[c] + 128 * (kind * len(tiles) + tiles.index(tile))
    raise ValueError


def kernel(
    ndp,
    nz,
    send_ref,
    take_ref,
    image_ref,
    owner_ref,
    qkv_hbm,
    cot_hbm,
    w_hbm,
    out_ref,
    grad_ref,
    qkv_v,
    cot_v,
    wpad,
    stage,
    recv,
    packed,
    bias,
    pcat,
    rhs,
    zsend,
    zrecv,
    fin,
    unpack,
    acc,
    inter,
    gcot,
    gctx,
    edge,
    gbuf,
    gdp_send,
    gdp_recv,
    gz_send,
    gz_recv,
    source_of,
    work_of,
    local_sem,
    y_send,
    y_recv,
    z_send,
    z_recv,
    x_send,
    x_recv,
    g_send,
    g_recv,
):
    p = lax.axis_index("dp")
    j = lax.axis_index("mp")
    z = lax.div(j, NX)
    x = lax.rem(j, NX)
    nb = ndp
    rows = nb * BR
    nmp = nz * NX
    arows = AROWS // ndp
    per_z = 2 * arows // nz

    def dp_peer(i):
        return lax.rem(p + i, ndp)

    def z_peer(i):
        return lax.rem(z + i, nz)

    def x_peer(i):
        return lax.rem(x + i, NX)

    qkv_copy = pltpu.make_async_copy(qkv_hbm, qkv_v, local_sem.at[0])
    cot_copy = pltpu.make_async_copy(cot_hbm, cot_v, local_sem.at[1])
    w_copy = pltpu.make_async_copy(w_hbm, wpad.at[pl.ds(64, D)], local_sem.at[2])
    qkv_copy.start()
    cot_copy.start()

    barrier = pltpu.get_barrier_semaphore()

    @pl.loop(1, ndp)
    def _(i):
        pl.semaphore_signal(barrier, inc=1, device_id=(dp_peer(i), j), device_id_type=MESH)

    @pl.loop(1, nz)
    def _(i):
        pl.semaphore_signal(barrier, inc=1, device_id=(p, z_peer(i) * NX + x), device_id_type=MESH)

    @pl.loop(1, NX)
    def _(i):
        pl.semaphore_signal(barrier, inc=1, device_id=(p, z * NX + x_peer(i)), device_id_type=MESH)

    @pl.loop(0, nb)
    def _(v):
        source, work = jnp.int32(0), jnp.int32(0)
        for s in range(nb):
            source = jnp.where(send_ref[s] == v, s, source)
            work = jnp.where(take_ref[s] == v, s, work)
        source_of[v] = source
        work_of[v] = work

    qkv_copy.wait()
    w_copy.start()
    pl.semaphore_wait(barrier, ndp + nz + NX - 3)

    def block_of(target, c):
        s = source_of[target]
        first, many = TILES[c][0] * 128, 128 * len(TILES[c])
        return [qkv_v[s, :, kind * D + first : kind * D + first + many] for kind in range(3)]

    def y_copy(c, target):
        columns = pl.ds(STARTS[c], WIDTHS[c])
        return pltpu.make_async_remote_copy(
            src_ref=stage.at[target, :, columns],
            dst_ref=recv.at[p, :, columns],
            send_sem=y_send.at[c],
            recv_sem=y_recv.at[c],
            device_id=(target, j),
            device_id_type=MESH,
        )

    def send_chunk(c):
        many = WIDTHS[c] // 3

        @pl.loop(1, ndp)
        def _(i):
            target = dp_peer(i)
            for kind, part in enumerate(block_of(target, c)):
                stage[target, :, STARTS[c] + kind * many : STARTS[c] + (kind + 1) * many] = part
            y_copy(c, target).start()

        for kind, part in enumerate(block_of(p, c)):
            recv[p, :, STARTS[c] + kind * many : STARTS[c] + (kind + 1) * many] = part

    send_chunk(0)

    cot_copy.wait()

    @pl.loop(0, nb // 2)
    def _(i):
        pair = [cot_v[work_of[2 * i + b]].astype(F32) for b in range(2)]
        gcot[x, pl.ds(pl.multiple_of(2 * BR * i, 2 * BR), 2 * BR), :] = jnp.concatenate(pair, axis=0).astype(BF16)

    def x_gather(buffer, which, target):
        return pltpu.make_async_remote_copy(
            src_ref=buffer.at[x],
            dst_ref=buffer.at[x],
            send_sem=g_send.at[which],
            recv_sem=g_recv.at[which],
            device_id=(p, z * NX + target),
            device_id_type=MESH,
        )

    @pl.loop(1, NX)
    def _(i):
        x_gather(gcot, 0, x_peer(i)).start()

    for c in range(1, CHUNKS):
        send_chunk(c)

    wpad[0:64, :] = jnp.zeros((64, D), BF16)
    wpad[64 + D : 128 + D, :] = jnp.zeros((64, D), BF16)
    acc[...] = jnp.zeros_like(acc)

    row = lax.broadcasted_iota(jnp.int32, (rows, rows), 0)
    lane = lax.broadcasted_iota(jnp.int32, (rows, rows), 1)
    image_row = jnp.zeros((rows, rows), jnp.int32)
    image_lane = jnp.zeros((rows, rows), jnp.int32)
    slot_row = jnp.zeros((rows, rows), jnp.int32)
    for v in range(nb):
        image = image_ref[work_of[v]]
        image_row = jnp.where(lax.div(row, BR) == v, image, image_row)
        image_lane = jnp.where(lax.div(lane, BR) == v, image, image_lane)
        slot_row = jnp.where(lax.div(row, BR) == v, take_ref[v], slot_row)
    bias[...] = jnp.where(image_row == image_lane, 0.0, -jnp.inf)

    to_slot = jnp.where(
        (slot_row == lax.div(lane, BR)) & (lax.rem(row, BR) == lax.rem(lane, BR)), 1.0, 0.0
    ).astype(BF16)
    target_lane = jnp.broadcast_to(owner_ref[...], (rows, rows)).astype(F32)
    target_row = jnp.transpose(target_lane)
    earlier = jnp.where((target_row == target_lane) & (row < lane), 1.0, 0.0)
    rank = jnp.sum(earlier, axis=0, keepdims=True)
    code_work = target_lane[0:1, :] * 4.0 + rank
    code = jnp.dot(jnp.broadcast_to(code_work, (16, rows)).astype(BF16), to_slot, preferred_element_type=F32)
    line = lax.broadcasted_iota(jnp.int32, (nmp * 8, rows), 0)
    part = lax.rem(line, 8)
    base = lax.div(line, 8) * 4
    code_a = jnp.where(part <= 2, base, jnp.where(part >= 5, base + 2, -1)).astype(F32)
    code_b = jnp.where((part >= 2) & (part <= 4), base + 1, -1).astype(F32)
    code_all = jnp.broadcast_to(code[0:1, :], (nmp * 8, rows))
    pcat[:, 0:rows] = jnp.where(code_a == code_all, 1.0, 0.0).astype(BF16)
    pcat[:, rows : 2 * rows] = jnp.where(code_b == code_all, 1.0, 0.0).astype(BF16)

    def tile(kind, t):
        start = place_of(kind, t)
        return packed[:, start : start + 128]

    def attend(c):
        columns = pl.ds(STARTS[c], WIDTHS[c])
        arrived = recv.at[pl.ds(0, ndp - 1), :, columns]
        pltpu.make_async_copy(arrived, arrived, y_recv.at[c]).wait()
        mine = slice(STARTS[c], STARTS[c] + WIDTHS[c])
        packed[:, mine] = recv[:, :, mine].astype(F32).reshape(rows, WIDTHS[c]).astype(BF16)
        first = c * CC // 128
        tiles = [jnp.zeros((rows, 128), F32) for _ in range(3)]
        column = lax.broadcasted_iota(jnp.int32, (rows, 128), 1)
        for h in range(c * HPC, (c + 1) * HPC):
            low = h * HEAD
            span = range(low // 128, (low + HEAD - 1) // 128 + 1)
            inside = [(column + 128 * t >= low) & (column + 128 * t < low + HEAD) for t in span]
            query = [tile(0, t) * jnp.where(m, 1.0, 0.0).astype(BF16) for t, m in zip(span, inside)]
            query = jnp.concatenate(query, axis=1) if len(query) > 1 else query[0]
            keys = [tile(1, t) for t in span]
            keys = jnp.concatenate(keys, axis=1) if len(keys) > 1 else keys[0]
            values = [tile(2, t) for t in span]
            values = jnp.concatenate(values, axis=1) if len(values) > 1 else values[0]
            scores = lax.dot_general(query, keys, (((1,), (1,)), ((), ())), preferred_element_type=F32)
            scores = scores * (1.0 / math.sqrt(HEAD)) + bias[...]
            weights = jnp.exp(scores - jnp.max(scores, axis=-1, keepdims=True))
            probs = (weights / jnp.sum(weights, axis=-1, keepdims=True)).astype(BF16)
            context = jnp.dot(probs, values, preferred_element_type=F32)
            for i, (t, m) in enumerate(zip(span, inside)):
                tiles[t - first] = jnp.where(m, context[:, 128 * i : 128 * i + 128], tiles[t - first])
        natural = jnp.concatenate(tiles, axis=1).astype(BF16)
        if c == 0:
            gctx[x, :, 0:256] = natural[:, 0:256]
            edge[...] = natural[:, 256:384]
        if c == 1:
            gctx[x, :, 256:384] = natural[:, 0:128] + edge[...]
            gctx[x, :, 384:640] = natural[:, 128:384]
        turned = pltpu.roll(natural.astype(F32), 64 if c % 2 == 0 else 384 - 64, axis=1).astype(BF16)
        a, b = (natural, turned) if c % 2 == 0 else (turned, natural)
        rhs[0:rows, :] = a
        rhs[rows : 2 * rows, 0:256] = b[:, 128:384]
        rhs[rows : 2 * rows, 256:384] = b[:, 0:128]
        placed = jnp.dot(pcat[...], rhs[...], preferred_element_type=F32)
        kind = lax.rem(lax.broadcasted_iota(jnp.int32, (nmp * 8, 128), 0), 8)
        zero = (kind == 0) | (kind == 3) | (kind == 5)
        one = (kind == 1) | (kind == 4) | (kind == 6)
        chosen = jnp.where(zero, placed[:, 0:128], jnp.where(one, placed[:, 128:256], placed[:, 256:384]))
        zsend[c] = chosen.reshape(nz, NX, 8, 128).astype(BF16)

        @pl.loop(1, nz)
        def _(i):
            z_copy(c, z_peer(i)).start()

        zrecv[c, z] = zsend[c, z]

    def z_copy(c, target):
        return pltpu.make_async_remote_copy(
            src_ref=zsend.at[c, target],
            dst_ref=zrecv.at[c, z],
            send_sem=z_send.at[c],
            recv_sem=z_recv.at[c],
            device_id=(p, target * NX + x),
            device_id_type=MESH,
        )

    def x_copy(c, target):
        return pltpu.make_async_remote_copy(
            src_ref=zrecv.at[c, :, target],
            dst_ref=fin.at[c, :, x],
            send_sem=x_send.at[c],
            recv_sem=x_recv.at[c],
            device_id=(p, z * NX + target),
            device_id_type=MESH,
        )

    def relay(c):
        arrived = zrecv.at[c, pl.ds(0, nz - 1)]
        pltpu.make_async_copy(arrived, arrived, z_recv.at[c]).wait()

        @pl.loop(1, NX)
        def _(i):
            x_copy(c, x_peer(i)).start()

        fin[c, :, x] = zrecv[c, :, x]

    def project(c):
        arrived = fin.at[c, :, pl.ds(0, NX - 1)]
        pltpu.make_async_copy(arrived, arrived, x_recv.at[c]).wait()
        unpack[...] = fin[c].astype(F32).reshape(nmp * 8, 128)
        s = [unpack[pl.ds(i, nmp, stride=8), :] for i in range(8)]
        low = lax.broadcasted_iota(jnp.int32, (nmp, 128), 1) < 64
        zeroth = jnp.concatenate([s[0], s[1], jnp.where(low, s[2], 0.0)], axis=1)
        second = jnp.concatenate([s[5], s[6], s[7]], axis=1)
        first = jnp.concatenate([jnp.where(low, 0.0, s[2]), s[3], s[4]], axis=1).astype(BF16)
        both = jnp.concatenate([zeroth, second], axis=0).astype(BF16)
        start = c * CC
        acc[0 : 2 * nmp, :] += jnp.dot(both, wpad[start + 64 : start + 448, :], preferred_element_type=F32)
        acc[2 * nmp : 3 * nmp, :] += jnp.dot(first, wpad[start : start + 384, :], preferred_element_type=F32)

    def gdp_copy(target):
        return pltpu.make_async_remote_copy(
            src_ref=gdp_send.at[target],
            dst_ref=gdp_recv.at[p],
            send_sem=g_send.at[2],
            recv_sem=g_recv.at[2],
            device_id=(target, j),
            device_id_type=MESH,
        )

    def gz_copy(target):
        return pltpu.make_async_remote_copy(
            src_ref=gz_send.at[target],
            dst_ref=gz_recv.at[z],
            send_sem=g_send.at[3],
            recv_sem=g_recv.at[3],
            device_id=(p, target * NX + x),
            device_id_type=MESH,
        )

    def send_context():
        @pl.loop(1, NX)
        def _(i):
            x_gather(gctx, 1, x_peer(i)).start()

    def gradient_product():
        for which, buffer in ((0, gcot), (1, gctx)):
            arrived = buffer.at[pl.ds(0, NX - 1)]
            pltpu.make_async_copy(arrived, arrived, g_recv.at[which]).wait()
        right = gcot[...].reshape(NX * rows, GW)
        for m in range(GW // 128):
            left = gctx[:, :, 128 * m : 128 * m + 128].reshape(NX * rows, 128)
            product = lax.dot_general(left, right, (((0,), (0,)), ((), ())), preferred_element_type=F32)
            for t in range(GW // 128):
                gbuf[t, 128 * m : 128 * m + 128, :] = product[:, 128 * t : 128 * t + 128]
        for k in range(NX):

            @pl.when(x == k)
            def _():
                for half in range(2):
                    start = 1600 * half + PIECE * k
                    tiles = [min(start // 128 + i, 24) for i in range(5)]
                    flat = [gbuf[t % 5, pl.ds(t // 5, AROWS, stride=5), :] for t in tiles]
                    flat = jnp.concatenate(flat, axis=1)
                    if start % 128:
                        flat = pltpu.roll(flat, 640 - start % 128, axis=1)
                    flat = flat[:, 0:PADDED].reshape(ndp, arows, PADDED).astype(BF16)
                    gdp_send[:, :, half * PADDED : (half + 1) * PADDED] = flat

        @pl.loop(1, ndp)
        def _(i):
            gdp_copy(dp_peer(i)).start()

        gdp_recv[p] = gdp_send[p]

    def gradient_over_dp():
        arrived = gdp_recv.at[pl.ds(0, ndp - 1)]
        pltpu.make_async_copy(arrived, arrived, g_recv.at[2]).wait()
        total = gdp_recv[0].astype(F32)
        for i in range(1, ndp):
            total = total + gdp_recv[i].astype(F32)
        for a in range(arows):
            for half in range(2):
                n = 2 * a + half
                gz_send[n // per_z, n % per_z : n % per_z + 1, :] = total[a : a + 1, half * PADDED : (half + 1) * PADDED]

        @pl.loop(1, nz)
        def _(i):
            gz_copy(z_peer(i)).start()

        gz_recv[z] = gz_send[z]

    def gradient_over_z():
        arrived = gz_recv.at[pl.ds(0, nz - 1)]
        pltpu.make_async_copy(arrived, arrived, g_recv.at[3]).wait()
        total = gz_recv[0]
        for i in range(1, nz):
            total = total + gz_recv[i]
        grad_ref[...] = total

    attend(0)
    attend(1)
    send_context()
    relay(0)
    attend(2)
    w_copy.wait()
    relay(1)
    gradient_product()
    project(0)
    attend(3)
    relay(2)
    project(1)
    gradient_over_dp()
    project(2)
    relay(3)
    gradient_over_z()
    project(3)

    for t in range(D // 128):
        for k, start in ((0, 0), (2, nmp), (1, 2 * nmp)):
            inter[t, pl.ds(k, nmp, stride=3), :] = acc[start : start + nmp, 128 * t : 128 * t + 128]
        out_ref[:, 128 * t : 128 * t + 128] = inter[t].astype(BF16)

    for c in range(CHUNKS):
        gone = stage.at[pl.ds(0, ndp - 1), :, pl.ds(STARTS[c], WIDTHS[c])]
        pltpu.make_async_copy(gone, gone, y_send.at[c]).wait()
        gone = zsend.at[c, pl.ds(0, nz - 1)]
        pltpu.make_async_copy(gone, gone, z_send.at[c]).wait()
        gone = zrecv.at[c, :, pl.ds(0, NX - 1)]
        pltpu.make_async_copy(gone, gone, x_send.at[c]).wait()
    for which, buffer, many in ((0, gcot, NX), (1, gctx, NX), (2, gdp_send, ndp), (3, gz_send, nz)):
        gone = buffer.at[pl.ds(0, many - 1)]
        pltpu.make_async_copy(gone, gone, g_send.at[which]).wait()


def solution(mesh):
    ndp, nmp = mesh.shape["dp"], mesh.shape["mp"]
    nz = nmp // NX
    nb = ndp
    rows = nb * BR
    arows = AROWS // ndp
    per_z = 2 * arows // nz

    def body(qkv, send_pos, recv_pos, block_image, owner, cotangent, out_weight):
        smem = pl.BlockSpec(memory_space=pltpu.SMEM)
        vmem = pl.BlockSpec(memory_space=pltpu.VMEM)
        hbm = pl.BlockSpec(memory_space=pl.ANY)
        delivered, gradient = pl.pallas_call(
            functools.partial(kernel, ndp, nz),
            out_shape=(
                jax.ShapeDtypeStruct((3 * nmp, D), BF16),
                jax.ShapeDtypeStruct((per_z, PADDED), F32),
            ),
            in_specs=[smem, smem, smem, vmem, hbm, hbm, hbm],
            out_specs=(vmem, vmem),
            scratch_shapes=[
                pltpu.VMEM((nb, BR, 3 * D), BF16),
                pltpu.VMEM((nb, BR, GW), BF16),
                pltpu.VMEM((D + 128, D), BF16),
                pltpu.VMEM((nb, BR, 3 * D), BF16),
                pltpu.VMEM((nb, BR, 3 * D), BF16),
                pltpu.VMEM((rows, 3 * D), BF16),
                pltpu.VMEM((rows, rows), F32),
                pltpu.VMEM((nmp * 8, 2 * rows), BF16),
                pltpu.VMEM((2 * rows, 384), BF16),
                pltpu.VMEM((CHUNKS, nz, NX, 8, 128), BF16),
                pltpu.VMEM((CHUNKS, nz, NX, 8, 128), BF16),
                pltpu.VMEM((CHUNKS, nz, NX, 8, 128), BF16),
                pltpu.VMEM((nmp * 8, 128), F32),
                pltpu.VMEM((3 * nmp, D), F32),
                pltpu.VMEM((D // 128, 3 * nmp, 128), F32),
                pltpu.VMEM((NX, rows, GW), BF16),
                pltpu.VMEM((NX, rows, GW), BF16),
                pltpu.VMEM((rows, 128), BF16),
                pltpu.VMEM((GW // 128, GW, 128), F32),
                pltpu.VMEM((ndp, arows, 2 * PADDED), BF16),
                pltpu.VMEM((ndp, arows, 2 * PADDED), BF16),
                pltpu.VMEM((nz, per_z, PADDED), F32),
                pltpu.VMEM((nz, per_z, PADDED), F32),
                pltpu.SMEM((nb,), jnp.int32),
                pltpu.SMEM((nb,), jnp.int32),
                pltpu.SemaphoreType.DMA((3,)),
                pltpu.SemaphoreType.DMA((CHUNKS,)),
                pltpu.SemaphoreType.DMA((CHUNKS,)),
                pltpu.SemaphoreType.DMA((CHUNKS,)),
                pltpu.SemaphoreType.DMA((CHUNKS,)),
                pltpu.SemaphoreType.DMA((CHUNKS,)),
                pltpu.SemaphoreType.DMA((CHUNKS,)),
                pltpu.SemaphoreType.DMA((4,)),
                pltpu.SemaphoreType.DMA((4,)),
            ],
            compiler_params=pltpu.CompilerParams(
                collective_id=0, has_side_effects=True, vmem_limit_bytes=40 * 2**20
            ),
        )(
            send_pos,
            recv_pos,
            block_image,
            owner.reshape(1, rows),
            qkv.reshape(nb, BR, 3 * D),
            cotangent.reshape(nb, BR, GW),
            out_weight,
        )
        return delivered, gradient[:, :PIECE].reshape(-1)

    placed = (
        P(("dp", "mp"), None),
        P(("dp", "mp")),
        P(("dp", "mp")),
        P(("dp", "mp")),
        P(("dp", "mp"), None),
        P(("dp", "mp"), None),
        P(),
    )
    return jax.shard_map(
        body,
        mesh=mesh,
        in_specs=placed,
        out_specs=(P(("dp", "mp"), None), P(("dp", "mp"))),
        check_vma=False,
    )
```

```python
import functools
import math

import jax
import jax.numpy as jnp
from jax import lax
from jax.experimental import pallas as pl
from jax.experimental.pallas import tpu as pltpu
from jax.sharding import PartitionSpec as P

MESH = pl.DeviceIdType.MESH
D = 1280
HEAD = 80
GW = 640
BR = 8
NX = 4
CHUNKS = 4
HPC = 4
CC = HPC * HEAD
TILES = ((0, 1, 2), (3, 4), (5, 6, 7), (8, 9))
WIDTHS = tuple(3 * 128 * len(t) for t in TILES)
STARTS = tuple(sum(WIDTHS[:c]) for c in range(CHUNKS))
AROWS = 128
PIECE = 400
PADDED = 512
F32 = jnp.float32
BF16 = jnp.bfloat16


def place_of(kind, tile):
    for c, tiles in enumerate(TILES):
        if tile in tiles:
            return STARTS[c] + 128 * (kind * len(tiles) + tiles.index(tile))
    raise ValueError


def kernel(
    ndp,
    nz,
    send_ref,
    take_ref,
    image_ref,
    owner_ref,
    qkv_hbm,
    cot_hbm,
    w_hbm,
    out_ref,
    grad_ref,
    qkv_v,
    cot_v,
    wpad,
    stage,
    recv,
    packed,
    bias,
    pcat,
    rhs,
    zsend,
    zrecv,
    fin,
    unpack,
    acc,
    inter,
    gcot,
    gctx,
    edge,
    gbuf,
    gdp_send,
    gdp_recv,
    gz_send,
    gz_recv,
    source_of,
    work_of,
    local_sem,
    y_send,
    y_recv,
    z_send,
    z_recv,
    x_send,
    x_recv,
    g_send,
    g_recv,
):
    p = lax.axis_index("dp")
    j = lax.axis_index("mp")
    z = lax.div(j, NX)
    x = lax.rem(j, NX)
    nb = ndp
    rows = nb * BR
    nmp = nz * NX
    arows = AROWS // ndp
    per_z = 2 * arows // nz

    def offset(i, n):
        return jnp.where(lax.rem(i, 2) == 1, n // 2 - lax.div(i, 2), n - n // 2 + lax.div(i, 2))

    def dp_peer(i):
        return lax.rem(p + offset(i, ndp), ndp)

    def z_peer(i):
        return lax.rem(z + offset(i, nz), nz)

    def x_peer(i):
        return lax.rem(x + i, NX)

    qkv_copy = pltpu.make_async_copy(qkv_hbm, qkv_v, local_sem.at[0])
    cot_copy = pltpu.make_async_copy(cot_hbm, cot_v, local_sem.at[1])
    w_copy = pltpu.make_async_copy(w_hbm, wpad.at[pl.ds(64, D)], local_sem.at[2])
    qkv_copy.start()
    cot_copy.start()

    barrier = pltpu.get_barrier_semaphore()

    @pl.loop(1, ndp)
    def _(i):
        pl.semaphore_signal(barrier, inc=1, device_id=(dp_peer(i), j), device_id_type=MESH)

    @pl.loop(1, nz)
    def _(i):
        pl.semaphore_signal(barrier, inc=1, device_id=(p, z_peer(i) * NX + x), device_id_type=MESH)

    @pl.loop(1, NX)
    def _(i):
        pl.semaphore_signal(barrier, inc=1, device_id=(p, z * NX + x_peer(i)), device_id_type=MESH)

    @pl.loop(0, nb)
    def _(v):
        source, work = jnp.int32(0), jnp.int32(0)
        for s in range(nb):
            source = jnp.where(send_ref[s] == v, s, source)
            work = jnp.where(take_ref[s] == v, s, work)
        source_of[v] = source
        work_of[v] = work

    qkv_copy.wait()
    w_copy.start()
    pl.semaphore_wait(barrier, ndp + nz + NX - 3)

    def block_of(target, c):
        s = source_of[target]
        first, many = TILES[c][0] * 128, 128 * len(TILES[c])
        return [qkv_v[s, :, kind * D + first : kind * D + first + many] for kind in range(3)]

    def y_copy(c, target):
        columns = pl.ds(STARTS[c], WIDTHS[c])
        return pltpu.make_async_remote_copy(
            src_ref=stage.at[target, :, columns],
            dst_ref=recv.at[p, :, columns],
            send_sem=y_send.at[c],
            recv_sem=y_recv.at[c],
            device_id=(target, j),
            device_id_type=MESH,
        )

    def send_chunk(c):
        many = WIDTHS[c] // 3

        @pl.loop(1, ndp)
        def _(i):
            target = dp_peer(i)
            for kind, part in enumerate(block_of(target, c)):
                stage[target, :, STARTS[c] + kind * many : STARTS[c] + (kind + 1) * many] = part
            y_copy(c, target).start()

        for kind, part in enumerate(block_of(p, c)):
            recv[p, :, STARTS[c] + kind * many : STARTS[c] + (kind + 1) * many] = part

    send_chunk(0)

    cot_copy.wait()

    @pl.loop(0, nb // 2)
    def _(i):
        pair = [cot_v[work_of[2 * i + b]].astype(F32) for b in range(2)]
        gcot[x, pl.ds(pl.multiple_of(2 * BR * i, 2 * BR), 2 * BR), :] = jnp.concatenate(pair, axis=0).astype(BF16)

    def x_gather(buffer, which, target):
        return pltpu.make_async_remote_copy(
            src_ref=buffer.at[x],
            dst_ref=buffer.at[x],
            send_sem=g_send.at[which],
            recv_sem=g_recv.at[which],
            device_id=(p, z * NX + target),
            device_id_type=MESH,
        )

    @pl.loop(1, NX)
    def _(i):
        x_gather(gcot, 0, x_peer(i)).start()

    for c in range(1, CHUNKS):
        send_chunk(c)

    wpad[0:64, :] = jnp.zeros((64, D), BF16)
    wpad[64 + D : 128 + D, :] = jnp.zeros((64, D), BF16)
    acc[...] = jnp.zeros_like(acc)

    row = lax.broadcasted_iota(jnp.int32, (rows, rows), 0)
    lane = lax.broadcasted_iota(jnp.int32, (rows, rows), 1)
    image_row = jnp.zeros((rows, rows), jnp.int32)
    image_lane = jnp.zeros((rows, rows), jnp.int32)
    slot_row = jnp.zeros((rows, rows), jnp.int32)
    for v in range(nb):
        image = image_ref[work_of[v]]
        image_row = jnp.where(lax.div(row, BR) == v, image, image_row)
        image_lane = jnp.where(lax.div(lane, BR) == v, image, image_lane)
        slot_row = jnp.where(lax.div(row, BR) == v, take_ref[v], slot_row)
    bias[...] = jnp.where(image_row == image_lane, 0.0, -jnp.inf)

    to_slot = jnp.where(
        (slot_row == lax.div(lane, BR)) & (lax.rem(row, BR) == lax.rem(lane, BR)), 1.0, 0.0
    ).astype(BF16)
    target_lane = jnp.broadcast_to(owner_ref[...], (rows, rows)).astype(F32)
    target_row = jnp.transpose(target_lane)
    earlier = jnp.where((target_row == target_lane) & (row < lane), 1.0, 0.0)
    rank = jnp.sum(earlier, axis=0, keepdims=True)
    code_work = target_lane[0:1, :] * 4.0 + rank
    code = jnp.dot(jnp.broadcast_to(code_work, (16, rows)).astype(BF16), to_slot, preferred_element_type=F32)
    line = lax.broadcasted_iota(jnp.int32, (nmp * 8, rows), 0)
    part = lax.rem(line, 8)
    base = lax.div(line, 8) * 4
    code_a = jnp.where(part <= 2, base, jnp.where(part >= 5, base + 2, -1)).astype(F32)
    code_b = jnp.where((part >= 2) & (part <= 4), base + 1, -1).astype(F32)
    code_all = jnp.broadcast_to(code[0:1, :], (nmp * 8, rows))
    pcat[:, 0:rows] = jnp.where(code_a == code_all, 1.0, 0.0).astype(BF16)
    pcat[:, rows : 2 * rows] = jnp.where(code_b == code_all, 1.0, 0.0).astype(BF16)

    def tile(kind, t):
        start = place_of(kind, t)
        return packed[:, start : start + 128]

    def attend(c):
        columns = pl.ds(STARTS[c], WIDTHS[c])
        arrived = recv.at[pl.ds(0, ndp - 1), :, columns]
        pltpu.make_async_copy(arrived, arrived, y_recv.at[c]).wait()
        if c == CHUNKS - 1:
            send_gradient()
        mine = slice(STARTS[c], STARTS[c] + WIDTHS[c])
        packed[:, mine] = recv[:, :, mine].astype(F32).reshape(rows, WIDTHS[c]).astype(BF16)
        first = c * CC // 128
        tiles = [jnp.zeros((rows, 128), F32) for _ in range(3)]
        column = lax.broadcasted_iota(jnp.int32, (rows, 128), 1)
        for h in range(c * HPC, (c + 1) * HPC):
            low = h * HEAD
            span = range(low // 128, (low + HEAD - 1) // 128 + 1)
            inside = [(column + 128 * t >= low) & (column + 128 * t < low + HEAD) for t in span]
            query = [tile(0, t) * jnp.where(m, 1.0, 0.0).astype(BF16) for t, m in zip(span, inside)]
            query = jnp.concatenate(query, axis=1) if len(query) > 1 else query[0]
            keys = [tile(1, t) for t in span]
            keys = jnp.concatenate(keys, axis=1) if len(keys) > 1 else keys[0]
            values = [tile(2, t) for t in span]
            values = jnp.concatenate(values, axis=1) if len(values) > 1 else values[0]
            scores = lax.dot_general(query, keys, (((1,), (1,)), ((), ())), preferred_element_type=F32)
            scores = scores * (1.0 / math.sqrt(HEAD)) + bias[...]
            weights = jnp.exp(scores - jnp.max(scores, axis=-1, keepdims=True))
            probs = (weights / jnp.sum(weights, axis=-1, keepdims=True)).astype(BF16)
            context = jnp.dot(probs, values, preferred_element_type=F32)
            for i, (t, m) in enumerate(zip(span, inside)):
                tiles[t - first] = jnp.where(m, context[:, 128 * i : 128 * i + 128], tiles[t - first])
        natural = jnp.concatenate(tiles, axis=1).astype(BF16)
        if c == 0:
            gctx[x, :, 0:256] = natural[:, 0:256]
            edge[...] = natural[:, 256:384]
        if c == 1:
            gctx[x, :, 256:384] = natural[:, 0:128] + edge[...]
            gctx[x, :, 384:640] = natural[:, 128:384]
        turned = pltpu.roll(natural.astype(F32), 64 if c % 2 == 0 else 384 - 64, axis=1).astype(BF16)
        a, b = (natural, turned) if c % 2 == 0 else (turned, natural)
        rhs[0:rows, :] = a
        rhs[rows : 2 * rows, 0:256] = b[:, 128:384]
        rhs[rows : 2 * rows, 256:384] = b[:, 0:128]
        placed = jnp.dot(pcat[...], rhs[...], preferred_element_type=F32)
        kind = lax.rem(lax.broadcasted_iota(jnp.int32, (nmp * 8, 128), 0), 8)
        zero = (kind == 0) | (kind == 3) | (kind == 5)
        one = (kind == 1) | (kind == 4) | (kind == 6)
        chosen = jnp.where(zero, placed[:, 0:128], jnp.where(one, placed[:, 128:256], placed[:, 256:384]))
        zsend[c] = chosen.reshape(nz, NX, 8, 128).astype(BF16)

        @pl.loop(1, nz)
        def _(i):
            z_copy(c, z_peer(i)).start()

        zrecv[c, z] = zsend[c, z]

    def z_copy(c, target):
        return pltpu.make_async_remote_copy(
            src_ref=zsend.at[c, target],
            dst_ref=zrecv.at[c, z],
            send_sem=z_send.at[c],
            recv_sem=z_recv.at[c],
            device_id=(p, target * NX + x),
            device_id_type=MESH,
        )

    def x_copy(c, target):
        return pltpu.make_async_remote_copy(
            src_ref=zrecv.at[c, :, target],
            dst_ref=fin.at[c, :, x],
            send_sem=x_send.at[c],
            recv_sem=x_recv.at[c],
            device_id=(p, z * NX + target),
            device_id_type=MESH,
        )

    def relay(c):
        arrived = zrecv.at[c, pl.ds(0, nz - 1)]
        pltpu.make_async_copy(arrived, arrived, z_recv.at[c]).wait()

        @pl.loop(1, NX)
        def _(i):
            x_copy(c, x_peer(i)).start()

        fin[c, :, x] = zrecv[c, :, x]

    def project(c):
        arrived = fin.at[c, :, pl.ds(0, NX - 1)]
        pltpu.make_async_copy(arrived, arrived, x_recv.at[c]).wait()
        unpack[...] = fin[c].astype(F32).reshape(nmp * 8, 128)
        s = [unpack[pl.ds(i, nmp, stride=8), :] for i in range(8)]
        low = lax.broadcasted_iota(jnp.int32, (nmp, 128), 1) < 64
        zeroth = jnp.concatenate([s[0], s[1], jnp.where(low, s[2], 0.0)], axis=1)
        second = jnp.concatenate([s[5], s[6], s[7]], axis=1)
        first = jnp.concatenate([jnp.where(low, 0.0, s[2]), s[3], s[4]], axis=1).astype(BF16)
        both = jnp.concatenate([zeroth, second], axis=0).astype(BF16)
        start = c * CC
        acc[0 : 2 * nmp, :] += jnp.dot(both, wpad[start + 64 : start + 448, :], preferred_element_type=F32)
        acc[2 * nmp : 3 * nmp, :] += jnp.dot(first, wpad[start : start + 384, :], preferred_element_type=F32)

    def gdp_copy(target):
        return pltpu.make_async_remote_copy(
            src_ref=gdp_send.at[target],
            dst_ref=gdp_recv.at[p],
            send_sem=g_send.at[2],
            recv_sem=g_recv.at[2],
            device_id=(target, j),
            device_id_type=MESH,
        )

    def gz_copy(target):
        return pltpu.make_async_remote_copy(
            src_ref=gz_send.at[target],
            dst_ref=gz_recv.at[z],
            send_sem=g_send.at[3],
            recv_sem=g_recv.at[3],
            device_id=(p, target * NX + x),
            device_id_type=MESH,
        )

    def send_context():
        @pl.loop(1, NX)
        def _(i):
            x_gather(gctx, 1, x_peer(i)).start()

    def gradient_product():
        for which, buffer in ((0, gcot), (1, gctx)):
            arrived = buffer.at[pl.ds(0, NX - 1)]
            pltpu.make_async_copy(arrived, arrived, g_recv.at[which]).wait()
        right = gcot[...].reshape(NX * rows, GW)
        for m in range(GW // 128):
            left = gctx[:, :, 128 * m : 128 * m + 128].reshape(NX * rows, 128)
            product = lax.dot_general(left, right, (((0,), (0,)), ((), ())), preferred_element_type=F32)
            for t in range(GW // 128):
                gbuf[t, 128 * m : 128 * m + 128, :] = product[:, 128 * t : 128 * t + 128]
        for k in range(NX):

            @pl.when(x == k)
            def _():
                for half in range(2):
                    start = 1600 * half + PIECE * k
                    tiles = [min(start // 128 + i, 24) for i in range(5)]
                    flat = [gbuf[t % 5, pl.ds(t // 5, AROWS, stride=5), :] for t in tiles]
                    flat = jnp.concatenate(flat, axis=1)
                    if start % 128:
                        flat = pltpu.roll(flat, 640 - start % 128, axis=1)
                    flat = flat[:, 0:PADDED].reshape(ndp, arows, PADDED).astype(BF16)
                    gdp_send[:, :, half * PADDED : (half + 1) * PADDED] = flat

        gdp_recv[p] = gdp_send[p]

    def send_gradient():
        @pl.loop(1, ndp)
        def _(i):
            gdp_copy(dp_peer(i)).start()

    def gradient_over_dp():
        arrived = gdp_recv.at[pl.ds(0, ndp - 1)]
        pltpu.make_async_copy(arrived, arrived, g_recv.at[2]).wait()
        total = gdp_recv[0].astype(F32)
        for i in range(1, ndp):
            total = total + gdp_recv[i].astype(F32)
        for a in range(arows):
            for half in range(2):
                n = 2 * a + half
                gz_send[n // per_z, n % per_z : n % per_z + 1, :] = total[a : a + 1, half * PADDED : (half + 1) * PADDED]

        @pl.loop(1, nz)
        def _(i):
            gz_copy(z_peer(i)).start()

        gz_recv[z] = gz_send[z]

    def gradient_over_z():
        arrived = gz_recv.at[pl.ds(0, nz - 1)]
        pltpu.make_async_copy(arrived, arrived, g_recv.at[3]).wait()
        total = gz_recv[0]
        for i in range(1, nz):
            total = total + gz_recv[i]
        grad_ref[...] = total

    attend(0)
    attend(1)
    send_context()
    relay(0)
    attend(2)
    w_copy.wait()
    relay(1)
    gradient_product()
    project(0)
    attend(3)
    relay(2)
    project(1)
    gradient_over_dp()
    project(2)
    relay(3)
    gradient_over_z()
    project(3)

    for t in range(D // 128):
        for k, start in ((0, 0), (2, nmp), (1, 2 * nmp)):
            inter[t, pl.ds(k, nmp, stride=3), :] = acc[start : start + nmp, 128 * t : 128 * t + 128]
        out_ref[:, 128 * t : 128 * t + 128] = inter[t].astype(BF16)

    for c in range(CHUNKS):
        gone = stage.at[pl.ds(0, ndp - 1), :, pl.ds(STARTS[c], WIDTHS[c])]
        pltpu.make_async_copy(gone, gone, y_send.at[c]).wait()
        gone = zsend.at[c, pl.ds(0, nz - 1)]
        pltpu.make_async_copy(gone, gone, z_send.at[c]).wait()
        gone = zrecv.at[c, :, pl.ds(0, NX - 1)]
        pltpu.make_async_copy(gone, gone, x_send.at[c]).wait()
    for which, buffer, many in ((0, gcot, NX), (1, gctx, NX), (2, gdp_send, ndp), (3, gz_send, nz)):
        gone = buffer.at[pl.ds(0, many - 1)]
        pltpu.make_async_copy(gone, gone, g_send.at[which]).wait()


def solution(mesh):
    ndp, nmp = mesh.shape["dp"], mesh.shape["mp"]
    nz = nmp // NX
    nb = ndp
    rows = nb * BR
    arows = AROWS // ndp
    per_z = 2 * arows // nz

    def body(qkv, send_pos, recv_pos, block_image, owner, cotangent, out_weight):
        smem = pl.BlockSpec(memory_space=pltpu.SMEM)
        vmem = pl.BlockSpec(memory_space=pltpu.VMEM)
        hbm = pl.BlockSpec(memory_space=pl.ANY)
        delivered, gradient = pl.pallas_call(
            functools.partial(kernel, ndp, nz),
            out_shape=(
                jax.ShapeDtypeStruct((3 * nmp, D), BF16),
                jax.ShapeDtypeStruct((per_z, PADDED), F32),
            ),
            in_specs=[smem, smem, smem, vmem, hbm, hbm, hbm],
            out_specs=(vmem, vmem),
            scratch_shapes=[
                pltpu.VMEM((nb, BR, 3 * D), BF16),
                pltpu.VMEM((nb, BR, GW), BF16),
                pltpu.VMEM((D + 128, D), BF16),
                pltpu.VMEM((nb, BR, 3 * D), BF16),
                pltpu.VMEM((nb, BR, 3 * D), BF16),
                pltpu.VMEM((rows, 3 * D), BF16),
                pltpu.VMEM((rows, rows), F32),
                pltpu.VMEM((nmp * 8, 2 * rows), BF16),
                pltpu.VMEM((2 * rows, 384), BF16),
                pltpu.VMEM((CHUNKS, nz, NX, 8, 128), BF16),
                pltpu.VMEM((CHUNKS, nz, NX, 8, 128), BF16),
                pltpu.VMEM((CHUNKS, nz, NX, 8, 128), BF16),
                pltpu.VMEM((nmp * 8, 128), F32),
                pltpu.VMEM((3 * nmp, D), F32),
                pltpu.VMEM((D // 128, 3 * nmp, 128), F32),
                pltpu.VMEM((NX, rows, GW), BF16),
                pltpu.VMEM((NX, rows, GW), BF16),
                pltpu.VMEM((rows, 128), BF16),
                pltpu.VMEM((GW // 128, GW, 128), F32),
                pltpu.VMEM((ndp, arows, 2 * PADDED), BF16),
                pltpu.VMEM((ndp, arows, 2 * PADDED), BF16),
                pltpu.VMEM((nz, per_z, PADDED), F32),
                pltpu.VMEM((nz, per_z, PADDED), F32),
                pltpu.SMEM((nb,), jnp.int32),
                pltpu.SMEM((nb,), jnp.int32),
                pltpu.SemaphoreType.DMA((3,)),
                pltpu.SemaphoreType.DMA((CHUNKS,)),
                pltpu.SemaphoreType.DMA((CHUNKS,)),
                pltpu.SemaphoreType.DMA((CHUNKS,)),
                pltpu.SemaphoreType.DMA((CHUNKS,)),
                pltpu.SemaphoreType.DMA((CHUNKS,)),
                pltpu.SemaphoreType.DMA((CHUNKS,)),
                pltpu.SemaphoreType.DMA((4,)),
                pltpu.SemaphoreType.DMA((4,)),
            ],
            compiler_params=pltpu.CompilerParams(
                collective_id=0, has_side_effects=True, vmem_limit_bytes=62 * 2**20
            ),
        )(
            send_pos,
            recv_pos,
            block_image,
            owner.reshape(1, rows),
            qkv.reshape(nb, BR, 3 * D),
            cotangent.reshape(nb, BR, GW),
            out_weight,
        )
        return delivered, gradient[:, :PIECE].reshape(-1)

    placed = (
        P(("dp", "mp"), None),
        P(("dp", "mp")),
        P(("dp", "mp")),
        P(("dp", "mp")),
        P(("dp", "mp"), None),
        P(("dp", "mp"), None),
        P(),
    )
    return jax.shard_map(
        body,
        mesh=mesh,
        in_specs=placed,
        out_specs=(P(("dp", "mp"), None), P(("dp", "mp"))),
        check_vma=False,
    )
```

```python
import functools
import math

import jax
import jax.numpy as jnp
from jax import lax
from jax.experimental import pallas as pl
from jax.experimental.pallas import tpu as pltpu
from jax.sharding import PartitionSpec as P

MESH = pl.DeviceIdType.MESH
D = 1280
HEAD = 80
GW = 640
BR = 8
NX = 4
CHUNKS = 4
HPC = 4
CC = HPC * HEAD
TILES = ((0, 1, 2), (3, 4), (5, 6, 7), (8, 9))
WIDTHS = tuple(3 * 128 * len(t) for t in TILES)
STARTS = tuple(sum(WIDTHS[:c]) for c in range(CHUNKS))
AROWS = 128
PIECE = 400
PADDED = 512
F32 = jnp.float32
BF16 = jnp.bfloat16


def place_of(kind, tile):
    for c, tiles in enumerate(TILES):
        if tile in tiles:
            return STARTS[c] + 128 * (kind * len(tiles) + tiles.index(tile))
    raise ValueError


def kernel(
    ndp,
    nz,
    send_hbm,
    take_hbm,
    image_hbm,
    owner_hbm,
    qkv_hbm,
    cot_hbm,
    w_hbm,
    out_ref,
    grad_ref,
    qkv_v,
    cot_v,
    wpad,
    stage,
    recv,
    packed,
    bias,
    pcat,
    rhs,
    zsend,
    zrecv,
    fin,
    unpack,
    acc,
    inter,
    gcot,
    gctx,
    edge,
    gbuf,
    gdp_send,
    gdp_recv,
    gz_send,
    gz_recv,
    send_ref,
    take_ref,
    image_ref,
    owner_ref,
    source_of,
    work_of,
    local_sem,
    y_send,
    y_recv,
    z_send,
    z_recv,
    x_send,
    x_recv,
    g_send,
    g_recv,
):
    p = lax.axis_index("dp")
    j = lax.axis_index("mp")
    z = lax.div(j, NX)
    x = lax.rem(j, NX)
    nb = ndp
    rows = nb * BR
    nmp = nz * NX
    arows = AROWS // ndp
    per_z = 2 * arows // nz

    def offset(i, n):
        return jnp.where(lax.rem(i, 2) == 1, n // 2 - lax.div(i, 2), n - n // 2 + lax.div(i, 2))

    def dp_peer(i):
        return lax.rem(p + offset(i, ndp), ndp)

    def z_peer(i):
        return lax.rem(z + offset(i, nz), nz)

    def x_peer(i):
        return lax.rem(x + i, NX)

    qkv_copy = pltpu.make_async_copy(qkv_hbm, qkv_v, local_sem.at[0])
    cot_copy = pltpu.make_async_copy(cot_hbm, cot_v, local_sem.at[1])
    w_copy = pltpu.make_async_copy(w_hbm, wpad.at[pl.ds(64, D)], local_sem.at[2])
    tables = [
        pltpu.make_async_copy(source, target, local_sem.at[3 + i])
        for i, (source, target) in enumerate(
            ((send_hbm, send_ref), (take_hbm, take_ref), (image_hbm, image_ref), (owner_hbm, owner_ref))
        )
    ]
    for copy in tables:
        copy.start()
    qkv_copy.start()
    cot_copy.start()

    barrier = pltpu.get_barrier_semaphore()

    @pl.loop(1, ndp)
    def _(i):
        pl.semaphore_signal(barrier, inc=1, device_id=(dp_peer(i), j), device_id_type=MESH)

    @pl.loop(1, nz)
    def _(i):
        pl.semaphore_signal(barrier, inc=1, device_id=(p, z_peer(i) * NX + x), device_id_type=MESH)

    @pl.loop(1, NX)
    def _(i):
        pl.semaphore_signal(barrier, inc=1, device_id=(p, z * NX + x_peer(i)), device_id_type=MESH)

    for copy in tables:
        copy.wait()

    @pl.loop(0, nb)
    def _(v):
        source, work = jnp.int32(0), jnp.int32(0)
        for s in range(nb):
            source = jnp.where(send_ref[s] == v, s, source)
            work = jnp.where(take_ref[s] == v, s, work)
        source_of[v] = source
        work_of[v] = work

    qkv_copy.wait()
    w_copy.start()
    pl.semaphore_wait(barrier, ndp + nz + NX - 3)

    def block_of(target, c):
        s = source_of[target]
        first, many = TILES[c][0] * 128, 128 * len(TILES[c])
        return [qkv_v[s, :, kind * D + first : kind * D + first + many] for kind in range(3)]

    def y_copy(c, target):
        columns = pl.ds(STARTS[c], WIDTHS[c])
        return pltpu.make_async_remote_copy(
            src_ref=stage.at[target, :, columns],
            dst_ref=recv.at[p, :, columns],
            send_sem=y_send.at[c],
            recv_sem=y_recv.at[c],
            device_id=(target, j),
            device_id_type=MESH,
        )

    def send_chunk(c):
        many = WIDTHS[c] // 3

        @pl.loop(1, ndp)
        def _(i):
            target = dp_peer(i)
            for kind, part in enumerate(block_of(target, c)):
                stage[target, :, STARTS[c] + kind * many : STARTS[c] + (kind + 1) * many] = part
            y_copy(c, target).start()

        for kind, part in enumerate(block_of(p, c)):
            recv[p, :, STARTS[c] + kind * many : STARTS[c] + (kind + 1) * many] = part

    send_chunk(0)

    cot_copy.wait()

    @pl.loop(0, nb // 2)
    def _(i):
        pair = [cot_v[work_of[2 * i + b]].astype(F32) for b in range(2)]
        gcot[x, pl.ds(pl.multiple_of(2 * BR * i, 2 * BR), 2 * BR), :] = jnp.concatenate(pair, axis=0).astype(BF16)

    def x_gather(buffer, which, target):
        return pltpu.make_async_remote_copy(
            src_ref=buffer.at[x],
            dst_ref=buffer.at[x],
            send_sem=g_send.at[which],
            recv_sem=g_recv.at[which],
            device_id=(p, z * NX + target),
            device_id_type=MESH,
        )

    @pl.loop(1, NX)
    def _(i):
        x_gather(gcot, 0, x_peer(i)).start()

    for c in range(1, CHUNKS):
        send_chunk(c)

    wpad[0:64, :] = jnp.zeros((64, D), BF16)
    wpad[64 + D : 128 + D, :] = jnp.zeros((64, D), BF16)
    acc[...] = jnp.zeros_like(acc)

    row = lax.broadcasted_iota(jnp.int32, (rows, rows), 0)
    lane = lax.broadcasted_iota(jnp.int32, (rows, rows), 1)
    image_row = jnp.zeros((rows, rows), jnp.int32)
    image_lane = jnp.zeros((rows, rows), jnp.int32)
    slot_row = jnp.zeros((rows, rows), jnp.int32)
    for v in range(nb):
        image = image_ref[work_of[v]]
        image_row = jnp.where(lax.div(row, BR) == v, image, image_row)
        image_lane = jnp.where(lax.div(lane, BR) == v, image, image_lane)
        slot_row = jnp.where(lax.div(row, BR) == v, take_ref[v], slot_row)
    bias[...] = jnp.where(image_row == image_lane, 0.0, -jnp.inf)

    to_slot = jnp.where(
        (slot_row == lax.div(lane, BR)) & (lax.rem(row, BR) == lax.rem(lane, BR)), 1.0, 0.0
    ).astype(BF16)
    target_lane = jnp.broadcast_to(owner_ref[...], (rows, rows)).astype(F32)
    target_row = jnp.transpose(target_lane)
    earlier = jnp.where((target_row == target_lane) & (row < lane), 1.0, 0.0)
    rank = jnp.sum(earlier, axis=0, keepdims=True)
    code_work = target_lane[0:1, :] * 4.0 + rank
    code = jnp.dot(jnp.broadcast_to(code_work, (16, rows)).astype(BF16), to_slot, preferred_element_type=F32)
    line = lax.broadcasted_iota(jnp.int32, (nmp * 8, rows), 0)
    part = lax.rem(line, 8)
    base = lax.div(line, 8) * 4
    code_a = jnp.where(part <= 2, base, jnp.where(part >= 5, base + 2, -1)).astype(F32)
    code_b = jnp.where((part >= 2) & (part <= 4), base + 1, -1).astype(F32)
    code_all = jnp.broadcast_to(code[0:1, :], (nmp * 8, rows))
    pcat[:, 0:rows] = jnp.where(code_a == code_all, 1.0, 0.0).astype(BF16)
    pcat[:, rows : 2 * rows] = jnp.where(code_b == code_all, 1.0, 0.0).astype(BF16)

    def tile(kind, t):
        start = place_of(kind, t)
        return packed[:, start : start + 128]

    def attend(c):
        columns = pl.ds(STARTS[c], WIDTHS[c])
        arrived = recv.at[pl.ds(0, ndp - 1), :, columns]
        pltpu.make_async_copy(arrived, arrived, y_recv.at[c]).wait()
        if c == CHUNKS - 1:
            send_gradient()
        mine = slice(STARTS[c], STARTS[c] + WIDTHS[c])
        packed[:, mine] = recv[:, :, mine].astype(F32).reshape(rows, WIDTHS[c]).astype(BF16)
        first = c * CC // 128
        tiles = [jnp.zeros((rows, 128), F32) for _ in range(3)]
        column = lax.broadcasted_iota(jnp.int32, (rows, 128), 1)
        for h in range(c * HPC, (c + 1) * HPC):
            low = h * HEAD
            span = range(low // 128, (low + HEAD - 1) // 128 + 1)
            inside = [(column + 128 * t >= low) & (column + 128 * t < low + HEAD) for t in span]
            query = [tile(0, t) * jnp.where(m, 1.0, 0.0).astype(BF16) for t, m in zip(span, inside)]
            query = jnp.concatenate(query, axis=1) if len(query) > 1 else query[0]
            keys = [tile(1, t) for t in span]
            keys = jnp.concatenate(keys, axis=1) if len(keys) > 1 else keys[0]
            values = [tile(2, t) for t in span]
            values = jnp.concatenate(values, axis=1) if len(values) > 1 else values[0]
            scores = lax.dot_general(query, keys, (((1,), (1,)), ((), ())), preferred_element_type=F32)
            scores = scores * (1.0 / math.sqrt(HEAD)) + bias[...]
            weights = jnp.exp(scores - jnp.max(scores, axis=-1, keepdims=True))
            probs = (weights / jnp.sum(weights, axis=-1, keepdims=True)).astype(BF16)
            context = jnp.dot(probs, values, preferred_element_type=F32)
            for i, (t, m) in enumerate(zip(span, inside)):
                tiles[t - first] = jnp.where(m, context[:, 128 * i : 128 * i + 128], tiles[t - first])
        natural = jnp.concatenate(tiles, axis=1).astype(BF16)
        if c == 0:
            gctx[x, :, 0:256] = natural[:, 0:256]
            edge[...] = natural[:, 256:384]
        if c == 1:
            gctx[x, :, 256:384] = natural[:, 0:128] + edge[...]
            gctx[x, :, 384:640] = natural[:, 128:384]
        turned = pltpu.roll(natural.astype(F32), 64 if c % 2 == 0 else 384 - 64, axis=1).astype(BF16)
        a, b = (natural, turned) if c % 2 == 0 else (turned, natural)
        rhs[0:rows, :] = a
        rhs[rows : 2 * rows, 0:256] = b[:, 128:384]
        rhs[rows : 2 * rows, 256:384] = b[:, 0:128]
        placed = jnp.dot(pcat[...], rhs[...], preferred_element_type=F32)
        kind = lax.rem(lax.broadcasted_iota(jnp.int32, (nmp * 8, 128), 0), 8)
        zero = (kind == 0) | (kind == 3) | (kind == 5)
        one = (kind == 1) | (kind == 4) | (kind == 6)
        chosen = jnp.where(zero, placed[:, 0:128], jnp.where(one, placed[:, 128:256], placed[:, 256:384]))
        zsend[c] = chosen.reshape(nz, NX, 8, 128).astype(BF16)

        @pl.loop(1, nz)
        def _(i):
            z_copy(c, z_peer(i)).start()

        zrecv[c, z] = zsend[c, z]

    def z_copy(c, target):
        return pltpu.make_async_remote_copy(
            src_ref=zsend.at[c, target],
            dst_ref=zrecv.at[c, z],
            send_sem=z_send.at[c],
            recv_sem=z_recv.at[c],
            device_id=(p, target * NX + x),
            device_id_type=MESH,
        )

    def x_copy(c, target):
        return pltpu.make_async_remote_copy(
            src_ref=zrecv.at[c, :, target],
            dst_ref=fin.at[c, :, x],
            send_sem=x_send.at[c],
            recv_sem=x_recv.at[c],
            device_id=(p, z * NX + target),
            device_id_type=MESH,
        )

    def relay(c):
        arrived = zrecv.at[c, pl.ds(0, nz - 1)]
        pltpu.make_async_copy(arrived, arrived, z_recv.at[c]).wait()

        @pl.loop(1, NX)
        def _(i):
            x_copy(c, x_peer(i)).start()

        fin[c, :, x] = zrecv[c, :, x]

    def project(c):
        arrived = fin.at[c, :, pl.ds(0, NX - 1)]
        pltpu.make_async_copy(arrived, arrived, x_recv.at[c]).wait()
        unpack[...] = fin[c].astype(F32).reshape(nmp * 8, 128)
        s = [unpack[pl.ds(i, nmp, stride=8), :] for i in range(8)]
        low = lax.broadcasted_iota(jnp.int32, (nmp, 128), 1) < 64
        zeroth = jnp.concatenate([s[0], s[1], jnp.where(low, s[2], 0.0)], axis=1)
        second = jnp.concatenate([s[5], s[6], s[7]], axis=1)
        first = jnp.concatenate([jnp.where(low, 0.0, s[2]), s[3], s[4]], axis=1).astype(BF16)
        both = jnp.concatenate([zeroth, second], axis=0).astype(BF16)
        start = c * CC
        acc[0 : 2 * nmp, :] += jnp.dot(both, wpad[start + 64 : start + 448, :], preferred_element_type=F32)
        acc[2 * nmp : 3 * nmp, :] += jnp.dot(first, wpad[start : start + 384, :], preferred_element_type=F32)

    def gdp_copy(target):
        return pltpu.make_async_remote_copy(
            src_ref=gdp_send.at[target],
            dst_ref=gdp_recv.at[p],
            send_sem=g_send.at[2],
            recv_sem=g_recv.at[2],
            device_id=(target, j),
            device_id_type=MESH,
        )

    def gz_copy(target):
        return pltpu.make_async_remote_copy(
            src_ref=gz_send.at[target],
            dst_ref=gz_recv.at[z],
            send_sem=g_send.at[3],
            recv_sem=g_recv.at[3],
            device_id=(p, target * NX + x),
            device_id_type=MESH,
        )

    def send_context():
        @pl.loop(1, NX)
        def _(i):
            x_gather(gctx, 1, x_peer(i)).start()

    def gradient_product():
        for which, buffer in ((0, gcot), (1, gctx)):
            arrived = buffer.at[pl.ds(0, NX - 1)]
            pltpu.make_async_copy(arrived, arrived, g_recv.at[which]).wait()
        right = gcot[...].reshape(NX * rows, GW)
        for m in range(GW // 128):
            left = gctx[:, :, 128 * m : 128 * m + 128].reshape(NX * rows, 128)
            product = lax.dot_general(left, right, (((0,), (0,)), ((), ())), preferred_element_type=F32)
            for t in range(GW // 128):
                gbuf[t, 128 * m : 128 * m + 128, :] = product[:, 128 * t : 128 * t + 128]
        for k in range(NX):

            @pl.when(x == k)
            def _():
                for half in range(2):
                    start = 1600 * half + PIECE * k
                    tiles = [min(start // 128 + i, 24) for i in range(5)]
                    flat = [gbuf[t % 5, pl.ds(t // 5, AROWS, stride=5), :] for t in tiles]
                    flat = jnp.concatenate(flat, axis=1)
                    if start % 128:
                        flat = pltpu.roll(flat, 640 - start % 128, axis=1)
                    flat = flat[:, 0:PADDED].reshape(ndp, arows, PADDED).astype(BF16)
                    gdp_send[:, :, half * PADDED : (half + 1) * PADDED] = flat

        gdp_recv[p] = gdp_send[p]

    def send_gradient():
        @pl.loop(1, ndp)
        def _(i):
            gdp_copy(dp_peer(i)).start()

    def gradient_over_dp():
        arrived = gdp_recv.at[pl.ds(0, ndp - 1)]
        pltpu.make_async_copy(arrived, arrived, g_recv.at[2]).wait()
        total = gdp_recv[0].astype(F32)
        for i in range(1, ndp):
            total = total + gdp_recv[i].astype(F32)
        for a in range(arows):
            for half in range(2):
                n = 2 * a + half
                gz_send[n // per_z, n % per_z : n % per_z + 1, :] = total[a : a + 1, half * PADDED : (half + 1) * PADDED]

        @pl.loop(1, nz)
        def _(i):
            gz_copy(z_peer(i)).start()

        gz_recv[z] = gz_send[z]

    def gradient_over_z():
        arrived = gz_recv.at[pl.ds(0, nz - 1)]
        pltpu.make_async_copy(arrived, arrived, g_recv.at[3]).wait()
        total = gz_recv[0]
        for i in range(1, nz):
            total = total + gz_recv[i]
        grad_ref[...] = total

    attend(0)
    attend(1)
    send_context()
    relay(0)
    attend(2)
    w_copy.wait()
    relay(1)
    gradient_product()
    project(0)
    attend(3)
    relay(2)
    project(1)
    gradient_over_dp()
    project(2)
    relay(3)
    gradient_over_z()
    project(3)

    for t in range(D // 128):
        for k, start in ((0, 0), (2, nmp), (1, 2 * nmp)):
            inter[t, pl.ds(k, nmp, stride=3), :] = acc[start : start + nmp, 128 * t : 128 * t + 128]
        out_ref[:, 128 * t : 128 * t + 128] = inter[t].astype(BF16)

    for c in range(CHUNKS):
        gone = stage.at[pl.ds(0, ndp - 1), :, pl.ds(STARTS[c], WIDTHS[c])]
        pltpu.make_async_copy(gone, gone, y_send.at[c]).wait()
        gone = zsend.at[c, pl.ds(0, nz - 1)]
        pltpu.make_async_copy(gone, gone, z_send.at[c]).wait()
        gone = zrecv.at[c, :, pl.ds(0, NX - 1)]
        pltpu.make_async_copy(gone, gone, x_send.at[c]).wait()
    for which, buffer, many in ((0, gcot, NX), (1, gctx, NX), (2, gdp_send, ndp), (3, gz_send, nz)):
        gone = buffer.at[pl.ds(0, many - 1)]
        pltpu.make_async_copy(gone, gone, g_send.at[which]).wait()


def hand_over(rows_ref, grad_ref, rows_out, grad_out, rows_v, grad_v, sems):
    inward = [
        pltpu.make_async_copy(rows_ref, rows_v, sems.at[0]),
        pltpu.make_async_copy(grad_ref, grad_v, sems.at[1]),
    ]
    outward = [
        pltpu.make_async_copy(rows_v, rows_out, sems.at[2]),
        pltpu.make_async_copy(grad_v, grad_out, sems.at[3]),
    ]
    for copy in inward:
        copy.start()
    for arrive, leave in zip(inward, outward):
        arrive.wait()
        leave.start()
    for copy in outward:
        copy.wait()


def solution(mesh):
    ndp, nmp = mesh.shape["dp"], mesh.shape["mp"]
    nz = nmp // NX
    nb = ndp
    rows = nb * BR
    arows = AROWS // ndp
    per_z = 2 * arows // nz

    def body(qkv, send_pos, recv_pos, block_image, owner, cotangent, out_weight):
        vmem = pl.BlockSpec(memory_space=pltpu.VMEM)
        hbm = pl.BlockSpec(memory_space=pltpu.HBM)
        delivered, gradient = pl.pallas_call(
            functools.partial(kernel, ndp, nz),
            out_shape=(
                jax.ShapeDtypeStruct((3 * nmp, D), BF16),
                jax.ShapeDtypeStruct((per_z, PADDED), F32),
            ),
            in_specs=[hbm] * 7,
            out_specs=(vmem, vmem),
            scratch_shapes=[
                pltpu.VMEM((nb, BR, 3 * D), BF16),
                pltpu.VMEM((nb, BR, GW), BF16),
                pltpu.VMEM((D + 128, D), BF16),
                pltpu.VMEM((nb, BR, 3 * D), BF16),
                pltpu.VMEM((nb, BR, 3 * D), BF16),
                pltpu.VMEM((rows, 3 * D), BF16),
                pltpu.VMEM((rows, rows), F32),
                pltpu.VMEM((nmp * 8, 2 * rows), BF16),
                pltpu.VMEM((2 * rows, 384), BF16),
                pltpu.VMEM((CHUNKS, nz, NX, 8, 128), BF16),
                pltpu.VMEM((CHUNKS, nz, NX, 8, 128), BF16),
                pltpu.VMEM((CHUNKS, nz, NX, 8, 128), BF16),
                pltpu.VMEM((nmp * 8, 128), F32),
                pltpu.VMEM((3 * nmp, D), F32),
                pltpu.VMEM((D // 128, 3 * nmp, 128), F32),
                pltpu.VMEM((NX, rows, GW), BF16),
                pltpu.VMEM((NX, rows, GW), BF16),
                pltpu.VMEM((rows, 128), BF16),
                pltpu.VMEM((GW // 128, GW, 128), F32),
                pltpu.VMEM((ndp, arows, 2 * PADDED), BF16),
                pltpu.VMEM((ndp, arows, 2 * PADDED), BF16),
                pltpu.VMEM((nz, per_z, PADDED), F32),
                pltpu.VMEM((nz, per_z, PADDED), F32),
                pltpu.SMEM((nb,), jnp.int32),
                pltpu.SMEM((nb,), jnp.int32),
                pltpu.SMEM((nb,), jnp.int32),
                pltpu.VMEM((1, rows), jnp.int32),
                pltpu.SMEM((nb,), jnp.int32),
                pltpu.SMEM((nb,), jnp.int32),
                pltpu.SemaphoreType.DMA((7,)),
                pltpu.SemaphoreType.DMA((CHUNKS,)),
                pltpu.SemaphoreType.DMA((CHUNKS,)),
                pltpu.SemaphoreType.DMA((CHUNKS,)),
                pltpu.SemaphoreType.DMA((CHUNKS,)),
                pltpu.SemaphoreType.DMA((CHUNKS,)),
                pltpu.SemaphoreType.DMA((CHUNKS,)),
                pltpu.SemaphoreType.DMA((4,)),
                pltpu.SemaphoreType.DMA((4,)),
            ],
            compiler_params=pltpu.CompilerParams(
                collective_id=0, has_side_effects=True, vmem_limit_bytes=62 * 2**20
            ),
        )(
            send_pos,
            recv_pos,
            block_image,
            owner.reshape(1, rows),
            qkv.reshape(nb, BR, 3 * D),
            cotangent.reshape(nb, BR, GW),
            out_weight,
        )
        delivered, gradient = pl.pallas_call(
            hand_over,
            out_shape=(
                jax.ShapeDtypeStruct(delivered.shape, BF16),
                jax.ShapeDtypeStruct(gradient.shape, F32),
            ),
            in_specs=[hbm, hbm],
            out_specs=(hbm, hbm),
            scratch_shapes=[
                pltpu.VMEM(delivered.shape, BF16),
                pltpu.VMEM(gradient.shape, F32),
                pltpu.SemaphoreType.DMA((4,)),
            ],
            compiler_params=pltpu.CompilerParams(vmem_limit_bytes=62 * 2**20),
        )(delivered, gradient)
        return delivered, gradient[:, :PIECE].reshape(-1)

    placed = (
        P(("dp", "mp"), None),
        P(("dp", "mp")),
        P(("dp", "mp")),
        P(("dp", "mp")),
        P(("dp", "mp"), None),
        P(("dp", "mp"), None),
        P(),
    )
    return jax.shard_map(
        body,
        mesh=mesh,
        in_specs=placed,
        out_specs=(P(("dp", "mp"), None), P(("dp", "mp"))),
        check_vma=False,
    )
```

```python
import functools
import math

import jax
import jax.numpy as jnp
from jax import lax
from jax.experimental import pallas as pl
from jax.experimental.pallas import tpu as pltpu
from jax.sharding import PartitionSpec as P

MESH = pl.DeviceIdType.MESH
D = 1280
HEAD = 80
GW = 640
BR = 8
NX = 4
CHUNKS = 4
HPC = 4
CC = HPC * HEAD
TILES = ((0, 1, 2), (3, 4), (5, 6, 7), (8, 9))
WIDTHS = tuple(3 * 128 * len(t) for t in TILES)
STARTS = tuple(sum(WIDTHS[:c]) for c in range(CHUNKS))
AROWS = 128
PIECE = 400
PADDED = 512
F32 = jnp.float32
BF16 = jnp.bfloat16


def place_of(kind, tile):
    for c, tiles in enumerate(TILES):
        if tile in tiles:
            return STARTS[c] + 128 * (kind * len(tiles) + tiles.index(tile))
    raise ValueError


def kernel(
    ndp,
    nz,
    send_hbm,
    take_hbm,
    image_hbm,
    owner_hbm,
    qkv_hbm,
    cot_hbm,
    w_hbm,
    out_ref,
    grad_ref,
    qkv_v,
    cot_v,
    wpad,
    stage,
    recv,
    packed,
    bias,
    pcat,
    rhs,
    zsend,
    zrecv,
    fin,
    unpack,
    acc,
    inter,
    gcot,
    gctx,
    edge,
    gbuf,
    gdp_send,
    gdp_recv,
    gz_send,
    gz_recv,
    send_ref,
    take_ref,
    image_ref,
    owner_ref,
    source_of,
    work_of,
    local_sem,
    y_send,
    y_recv,
    z_send,
    z_recv,
    x_send,
    x_recv,
    g_send,
    g_recv,
):
    p = lax.axis_index("dp")
    j = lax.axis_index("mp")
    z = lax.div(j, NX)
    x = lax.rem(j, NX)
    nb = ndp
    rows = nb * BR
    nmp = nz * NX
    arows = AROWS // ndp
    per_z = 2 * arows // nz

    def offset(i, n):
        return jnp.where(lax.rem(i, 2) == 1, n // 2 - lax.div(i, 2), n - n // 2 + lax.div(i, 2))

    def dp_peer(i):
        return lax.rem(p + offset(i, ndp), ndp)

    def z_peer(i):
        return lax.rem(z + offset(i, nz), nz)

    def x_peer(i):
        return lax.rem(x + offset(i, NX), NX)

    qkv_copy = pltpu.make_async_copy(qkv_hbm, qkv_v, local_sem.at[0])
    cot_copy = pltpu.make_async_copy(cot_hbm, cot_v, local_sem.at[1])
    w_copy = pltpu.make_async_copy(w_hbm, wpad.at[pl.ds(64, D)], local_sem.at[2])
    tables = [
        pltpu.make_async_copy(source, target, local_sem.at[3 + i])
        for i, (source, target) in enumerate(
            ((send_hbm, send_ref), (take_hbm, take_ref), (image_hbm, image_ref), (owner_hbm, owner_ref))
        )
    ]
    for copy in tables:
        copy.start()
    qkv_copy.start()
    cot_copy.start()

    barrier = pltpu.get_barrier_semaphore()

    @pl.loop(1, ndp)
    def _(i):
        pl.semaphore_signal(barrier, inc=1, device_id=(dp_peer(i), j), device_id_type=MESH)

    @pl.loop(1, nz)
    def _(i):
        pl.semaphore_signal(barrier, inc=1, device_id=(p, z_peer(i) * NX + x), device_id_type=MESH)

    @pl.loop(1, NX)
    def _(i):
        pl.semaphore_signal(barrier, inc=1, device_id=(p, z * NX + x_peer(i)), device_id_type=MESH)

    for copy in tables:
        copy.wait()

    @pl.loop(0, nb)
    def _(v):
        source, work = jnp.int32(0), jnp.int32(0)
        for s in range(nb):
            source = jnp.where(send_ref[s] == v, s, source)
            work = jnp.where(take_ref[s] == v, s, work)
        source_of[v] = source
        work_of[v] = work

    qkv_copy.wait()
    w_copy.start()
    pl.semaphore_wait(barrier, ndp + nz + NX - 3)

    def block_of(target, c):
        s = source_of[target]
        first, many = TILES[c][0] * 128, 128 * len(TILES[c])
        return [qkv_v[s, :, kind * D + first : kind * D + first + many] for kind in range(3)]

    def y_copy(c, target):
        columns = pl.ds(STARTS[c], WIDTHS[c])
        return pltpu.make_async_remote_copy(
            src_ref=stage.at[target, :, columns],
            dst_ref=recv.at[p, :, columns],
            send_sem=y_send.at[c],
            recv_sem=y_recv.at[c],
            device_id=(target, j),
            device_id_type=MESH,
        )

    def send_chunk(c):
        many = WIDTHS[c] // 3

        @pl.loop(1, ndp)
        def _(i):
            target = dp_peer(i)
            for kind, part in enumerate(block_of(target, c)):
                stage[target, :, STARTS[c] + kind * many : STARTS[c] + (kind + 1) * many] = part
            y_copy(c, target).start()

        for kind, part in enumerate(block_of(p, c)):
            recv[p, :, STARTS[c] + kind * many : STARTS[c] + (kind + 1) * many] = part

    send_chunk(0)

    cot_copy.wait()

    @pl.loop(0, nb // 2)
    def _(i):
        pair = [cot_v[work_of[2 * i + b]].astype(F32) for b in range(2)]
        gcot[x, pl.ds(pl.multiple_of(2 * BR * i, 2 * BR), 2 * BR), :] = jnp.concatenate(pair, axis=0).astype(BF16)

    def x_gather(buffer, which, target):
        return pltpu.make_async_remote_copy(
            src_ref=buffer.at[x],
            dst_ref=buffer.at[x],
            send_sem=g_send.at[which],
            recv_sem=g_recv.at[which],
            device_id=(p, z * NX + target),
            device_id_type=MESH,
        )

    @pl.loop(1, NX)
    def _(i):
        x_gather(gcot, 0, x_peer(i)).start()

    for c in range(1, CHUNKS):
        send_chunk(c)

    wpad[0:64, :] = jnp.zeros((64, D), BF16)
    wpad[64 + D : 128 + D, :] = jnp.zeros((64, D), BF16)
    acc[...] = jnp.zeros_like(acc)

    row = lax.broadcasted_iota(jnp.int32, (rows, rows), 0)
    lane = lax.broadcasted_iota(jnp.int32, (rows, rows), 1)
    image_row = jnp.zeros((rows, rows), jnp.int32)
    image_lane = jnp.zeros((rows, rows), jnp.int32)
    slot_row = jnp.zeros((rows, rows), jnp.int32)
    for v in range(nb):
        image = image_ref[work_of[v]]
        image_row = jnp.where(lax.div(row, BR) == v, image, image_row)
        image_lane = jnp.where(lax.div(lane, BR) == v, image, image_lane)
        slot_row = jnp.where(lax.div(row, BR) == v, take_ref[v], slot_row)
    bias[...] = jnp.where(image_row == image_lane, 0.0, -jnp.inf)

    to_slot = jnp.where(
        (slot_row == lax.div(lane, BR)) & (lax.rem(row, BR) == lax.rem(lane, BR)), 1.0, 0.0
    ).astype(BF16)
    target_lane = jnp.broadcast_to(owner_ref[...], (rows, rows)).astype(F32)
    target_row = jnp.transpose(target_lane)
    earlier = jnp.where((target_row == target_lane) & (row < lane), 1.0, 0.0)
    rank = jnp.sum(earlier, axis=0, keepdims=True)
    code_work = target_lane[0:1, :] * 4.0 + rank
    code = jnp.dot(jnp.broadcast_to(code_work, (16, rows)).astype(BF16), to_slot, preferred_element_type=F32)
    line = lax.broadcasted_iota(jnp.int32, (nmp * 8, rows), 0)
    part = lax.rem(line, 8)
    base = lax.div(line, 8) * 4
    code_a = jnp.where(part <= 2, base, jnp.where(part >= 5, base + 2, -1)).astype(F32)
    code_b = jnp.where((part >= 2) & (part <= 4), base + 1, -1).astype(F32)
    code_all = jnp.broadcast_to(code[0:1, :], (nmp * 8, rows))
    pcat[:, 0:rows] = jnp.where(code_a == code_all, 1.0, 0.0).astype(BF16)
    pcat[:, rows : 2 * rows] = jnp.where(code_b == code_all, 1.0, 0.0).astype(BF16)

    def tile(kind, t):
        start = place_of(kind, t)
        return packed[:, start : start + 128]

    def attend(c):
        columns = pl.ds(STARTS[c], WIDTHS[c])
        arrived = recv.at[pl.ds(0, ndp - 1), :, columns]
        pltpu.make_async_copy(arrived, arrived, y_recv.at[c]).wait()
        if c == CHUNKS - 1:
            send_gradient()
        mine = slice(STARTS[c], STARTS[c] + WIDTHS[c])
        packed[:, mine] = recv[:, :, mine].astype(F32).reshape(rows, WIDTHS[c]).astype(BF16)
        first = c * CC // 128
        tiles = [jnp.zeros((rows, 128), F32) for _ in range(3)]
        column = lax.broadcasted_iota(jnp.int32, (rows, 128), 1)
        for h in range(c * HPC, (c + 1) * HPC):
            low = h * HEAD
            span = range(low // 128, (low + HEAD - 1) // 128 + 1)
            inside = [(column + 128 * t >= low) & (column + 128 * t < low + HEAD) for t in span]
            query = [tile(0, t) * jnp.where(m, 1.0, 0.0).astype(BF16) for t, m in zip(span, inside)]
            query = jnp.concatenate(query, axis=1) if len(query) > 1 else query[0]
            keys = [tile(1, t) for t in span]
            keys = jnp.concatenate(keys, axis=1) if len(keys) > 1 else keys[0]
            values = [tile(2, t) for t in span]
            values = jnp.concatenate(values, axis=1) if len(values) > 1 else values[0]
            scores = lax.dot_general(query, keys, (((1,), (1,)), ((), ())), preferred_element_type=F32)
            scores = scores * (1.0 / math.sqrt(HEAD)) + bias[...]
            weights = jnp.exp(scores - jnp.max(scores, axis=-1, keepdims=True))
            probs = (weights / jnp.sum(weights, axis=-1, keepdims=True)).astype(BF16)
            context = jnp.dot(probs, values, preferred_element_type=F32)
            for i, (t, m) in enumerate(zip(span, inside)):
                tiles[t - first] = jnp.where(m, context[:, 128 * i : 128 * i + 128], tiles[t - first])
        natural = jnp.concatenate(tiles, axis=1).astype(BF16)
        if c == 0:
            gctx[x, :, 0:256] = natural[:, 0:256]
            edge[...] = natural[:, 256:384]
        if c == 1:
            gctx[x, :, 256:384] = natural[:, 0:128] + edge[...]
            gctx[x, :, 384:640] = natural[:, 128:384]
        turned = pltpu.roll(natural.astype(F32), 64 if c % 2 == 0 else 384 - 64, axis=1).astype(BF16)
        a, b = (natural, turned) if c % 2 == 0 else (turned, natural)
        rhs[0:rows, :] = a
        rhs[rows : 2 * rows, 0:256] = b[:, 128:384]
        rhs[rows : 2 * rows, 256:384] = b[:, 0:128]
        placed = jnp.dot(pcat[...], rhs[...], preferred_element_type=F32)
        kind = lax.rem(lax.broadcasted_iota(jnp.int32, (nmp * 8, 128), 0), 8)
        zero = (kind == 0) | (kind == 3) | (kind == 5)
        one = (kind == 1) | (kind == 4) | (kind == 6)
        chosen = jnp.where(zero, placed[:, 0:128], jnp.where(one, placed[:, 128:256], placed[:, 256:384]))
        zsend[c] = chosen.reshape(nz, NX, 8, 128).astype(BF16)

        @pl.loop(1, nz)
        def _(i):
            z_copy(c, z_peer(i)).start()

        zrecv[c, z] = zsend[c, z]

    def z_copy(c, target):
        return pltpu.make_async_remote_copy(
            src_ref=zsend.at[c, target],
            dst_ref=zrecv.at[c, z],
            send_sem=z_send.at[c],
            recv_sem=z_recv.at[c],
            device_id=(p, target * NX + x),
            device_id_type=MESH,
        )

    def x_copy(c, target):
        return pltpu.make_async_remote_copy(
            src_ref=zrecv.at[c, :, target],
            dst_ref=fin.at[c, :, x],
            send_sem=x_send.at[c],
            recv_sem=x_recv.at[c],
            device_id=(p, z * NX + target),
            device_id_type=MESH,
        )

    def relay(c):
        arrived = zrecv.at[c, pl.ds(0, nz - 1)]
        pltpu.make_async_copy(arrived, arrived, z_recv.at[c]).wait()

        @pl.loop(1, NX)
        def _(i):
            x_copy(c, x_peer(i)).start()

        fin[c, :, x] = zrecv[c, :, x]

    def project(c):
        arrived = fin.at[c, :, pl.ds(0, NX - 1)]
        pltpu.make_async_copy(arrived, arrived, x_recv.at[c]).wait()
        unpack[...] = fin[c].astype(F32).reshape(nmp * 8, 128)
        s = [unpack[pl.ds(i, nmp, stride=8), :] for i in range(8)]
        low = lax.broadcasted_iota(jnp.int32, (nmp, 128), 1) < 64
        zeroth = jnp.concatenate([s[0], s[1], jnp.where(low, s[2], 0.0)], axis=1)
        second = jnp.concatenate([s[5], s[6], s[7]], axis=1)
        first = jnp.concatenate([jnp.where(low, 0.0, s[2]), s[3], s[4]], axis=1).astype(BF16)
        both = jnp.concatenate([zeroth, second], axis=0).astype(BF16)
        start = c * CC
        acc[0 : 2 * nmp, :] += jnp.dot(both, wpad[start + 64 : start + 448, :], preferred_element_type=F32)
        acc[2 * nmp : 3 * nmp, :] += jnp.dot(first, wpad[start : start + 384, :], preferred_element_type=F32)

    def gdp_copy(target):
        return pltpu.make_async_remote_copy(
            src_ref=gdp_send.at[target],
            dst_ref=gdp_recv.at[p],
            send_sem=g_send.at[2],
            recv_sem=g_recv.at[2],
            device_id=(target, j),
            device_id_type=MESH,
        )

    def gz_copy(target):
        return pltpu.make_async_remote_copy(
            src_ref=gz_send.at[target],
            dst_ref=gz_recv.at[z],
            send_sem=g_send.at[3],
            recv_sem=g_recv.at[3],
            device_id=(p, target * NX + x),
            device_id_type=MESH,
        )

    def send_context():
        @pl.loop(1, NX)
        def _(i):
            x_gather(gctx, 1, x_peer(i)).start()

    def gradient_product():
        for which, buffer in ((0, gcot), (1, gctx)):
            arrived = buffer.at[pl.ds(0, NX - 1)]
            pltpu.make_async_copy(arrived, arrived, g_recv.at[which]).wait()
        right = gcot[...].reshape(NX * rows, GW)
        for m in range(GW // 128):
            left = gctx[:, :, 128 * m : 128 * m + 128].reshape(NX * rows, 128)
            product = lax.dot_general(left, right, (((0,), (0,)), ((), ())), preferred_element_type=F32)
            for t in range(GW // 128):
                gbuf[t, 128 * m : 128 * m + 128, :] = product[:, 128 * t : 128 * t + 128]
        for k in range(NX):

            @pl.when(x == k)
            def _():
                for half in range(2):
                    start = 1600 * half + PIECE * k
                    tiles = [min(start // 128 + i, 24) for i in range(5)]
                    flat = [gbuf[t % 5, pl.ds(t // 5, AROWS, stride=5), :] for t in tiles]
                    flat = jnp.concatenate(flat, axis=1)
                    if start % 128:
                        flat = pltpu.roll(flat, 640 - start % 128, axis=1)
                    flat = flat[:, 0:PADDED].reshape(ndp, arows, PADDED).astype(BF16)
                    gdp_send[:, :, half * PADDED : (half + 1) * PADDED] = flat

        gdp_recv[p] = gdp_send[p]

    def send_gradient():
        @pl.loop(1, ndp)
        def _(i):
            gdp_copy(dp_peer(i)).start()

    def gradient_over_dp():
        arrived = gdp_recv.at[pl.ds(0, ndp - 1)]
        pltpu.make_async_copy(arrived, arrived, g_recv.at[2]).wait()
        total = gdp_recv[0].astype(F32)
        for i in range(1, ndp):
            total = total + gdp_recv[i].astype(F32)
        for a in range(arows):
            for half in range(2):
                n = 2 * a + half
                gz_send[n // per_z, n % per_z : n % per_z + 1, :] = total[a : a + 1, half * PADDED : (half + 1) * PADDED]

        @pl.loop(1, nz)
        def _(i):
            gz_copy(z_peer(i)).start()

        gz_recv[z] = gz_send[z]

    def gradient_over_z():
        arrived = gz_recv.at[pl.ds(0, nz - 1)]
        pltpu.make_async_copy(arrived, arrived, g_recv.at[3]).wait()
        total = gz_recv[0]
        for i in range(1, nz):
            total = total + gz_recv[i]
        grad_ref[...] = total

    attend(0)
    attend(1)
    send_context()
    relay(0)
    attend(2)
    w_copy.wait()
    relay(1)
    gradient_product()
    project(0)
    attend(3)
    relay(2)
    project(1)
    gradient_over_dp()
    project(2)
    relay(3)
    gradient_over_z()
    project(3)

    for t in range(D // 128):
        for k, start in ((0, 0), (2, nmp), (1, 2 * nmp)):
            inter[t, pl.ds(k, nmp, stride=3), :] = acc[start : start + nmp, 128 * t : 128 * t + 128]
        out_ref[:, 128 * t : 128 * t + 128] = inter[t].astype(BF16)

    for c in range(CHUNKS):
        gone = stage.at[pl.ds(0, ndp - 1), :, pl.ds(STARTS[c], WIDTHS[c])]
        pltpu.make_async_copy(gone, gone, y_send.at[c]).wait()
        gone = zsend.at[c, pl.ds(0, nz - 1)]
        pltpu.make_async_copy(gone, gone, z_send.at[c]).wait()
        gone = zrecv.at[c, :, pl.ds(0, NX - 1)]
        pltpu.make_async_copy(gone, gone, x_send.at[c]).wait()
    for which, buffer, many in ((0, gcot, NX), (1, gctx, NX), (2, gdp_send, ndp), (3, gz_send, nz)):
        gone = buffer.at[pl.ds(0, many - 1)]
        pltpu.make_async_copy(gone, gone, g_send.at[which]).wait()


def hand_over(rows_ref, grad_ref, rows_out, grad_out, rows_v, grad_v, sems):
    inward = [
        pltpu.make_async_copy(rows_ref, rows_v, sems.at[0]),
        pltpu.make_async_copy(grad_ref, grad_v, sems.at[1]),
    ]
    outward = [
        pltpu.make_async_copy(rows_v, rows_out, sems.at[2]),
        pltpu.make_async_copy(grad_v, grad_out, sems.at[3]),
    ]
    for copy in inward:
        copy.start()
    for arrive, leave in zip(inward, outward):
        arrive.wait()
        leave.start()
    for copy in outward:
        copy.wait()


def solution(mesh):
    ndp, nmp = mesh.shape["dp"], mesh.shape["mp"]
    nz = nmp // NX
    nb = ndp
    rows = nb * BR
    arows = AROWS // ndp
    per_z = 2 * arows // nz

    def body(qkv, send_pos, recv_pos, block_image, owner, cotangent, out_weight):
        vmem = pl.BlockSpec(memory_space=pltpu.VMEM)
        hbm = pl.BlockSpec(memory_space=pltpu.HBM)
        delivered, gradient = pl.pallas_call(
            functools.partial(kernel, ndp, nz),
            out_shape=(
                jax.ShapeDtypeStruct((3 * nmp, D), BF16),
                jax.ShapeDtypeStruct((per_z, PADDED), F32),
            ),
            in_specs=[hbm] * 7,
            out_specs=(vmem, vmem),
            scratch_shapes=[
                pltpu.VMEM((nb, BR, 3 * D), BF16),
                pltpu.VMEM((nb, BR, GW), BF16),
                pltpu.VMEM((D + 128, D), BF16),
                pltpu.VMEM((nb, BR, 3 * D), BF16),
                pltpu.VMEM((nb, BR, 3 * D), BF16),
                pltpu.VMEM((rows, 3 * D), BF16),
                pltpu.VMEM((rows, rows), F32),
                pltpu.VMEM((nmp * 8, 2 * rows), BF16),
                pltpu.VMEM((2 * rows, 384), BF16),
                pltpu.VMEM((CHUNKS, nz, NX, 8, 128), BF16),
                pltpu.VMEM((CHUNKS, nz, NX, 8, 128), BF16),
                pltpu.VMEM((CHUNKS, nz, NX, 8, 128), BF16),
                pltpu.VMEM((nmp * 8, 128), F32),
                pltpu.VMEM((3 * nmp, D), F32),
                pltpu.VMEM((D // 128, 3 * nmp, 128), F32),
                pltpu.VMEM((NX, rows, GW), BF16),
                pltpu.VMEM((NX, rows, GW), BF16),
                pltpu.VMEM((rows, 128), BF16),
                pltpu.VMEM((GW // 128, GW, 128), F32),
                pltpu.VMEM((ndp, arows, 2 * PADDED), BF16),
                pltpu.VMEM((ndp, arows, 2 * PADDED), BF16),
                pltpu.VMEM((nz, per_z, PADDED), F32),
                pltpu.VMEM((nz, per_z, PADDED), F32),
                pltpu.SMEM((nb,), jnp.int32),
                pltpu.SMEM((nb,), jnp.int32),
                pltpu.SMEM((nb,), jnp.int32),
                pltpu.VMEM((1, rows), jnp.int32),
                pltpu.SMEM((nb,), jnp.int32),
                pltpu.SMEM((nb,), jnp.int32),
                pltpu.SemaphoreType.DMA((7,)),
                pltpu.SemaphoreType.DMA((CHUNKS,)),
                pltpu.SemaphoreType.DMA((CHUNKS,)),
                pltpu.SemaphoreType.DMA((CHUNKS,)),
                pltpu.SemaphoreType.DMA((CHUNKS,)),
                pltpu.SemaphoreType.DMA((CHUNKS,)),
                pltpu.SemaphoreType.DMA((CHUNKS,)),
                pltpu.SemaphoreType.DMA((4,)),
                pltpu.SemaphoreType.DMA((4,)),
            ],
            compiler_params=pltpu.CompilerParams(
                collective_id=0, has_side_effects=True, vmem_limit_bytes=62 * 2**20
            ),
        )(
            send_pos,
            recv_pos,
            block_image,
            owner.reshape(1, rows),
            qkv.reshape(nb, BR, 3 * D),
            cotangent.reshape(nb, BR, GW),
            out_weight,
        )
        delivered, gradient = pl.pallas_call(
            hand_over,
            out_shape=(
                jax.ShapeDtypeStruct(delivered.shape, BF16),
                jax.ShapeDtypeStruct(gradient.shape, F32),
            ),
            in_specs=[hbm, hbm],
            out_specs=(hbm, hbm),
            scratch_shapes=[
                pltpu.VMEM(delivered.shape, BF16),
                pltpu.VMEM(gradient.shape, F32),
                pltpu.SemaphoreType.DMA((4,)),
            ],
            compiler_params=pltpu.CompilerParams(vmem_limit_bytes=62 * 2**20),
        )(delivered, gradient)
        return delivered, gradient[:, :PIECE].reshape(-1)

    placed = (
        P(("dp", "mp"), None),
        P(("dp", "mp")),
        P(("dp", "mp")),
        P(("dp", "mp")),
        P(("dp", "mp"), None),
        P(("dp", "mp"), None),
        P(),
    )
    return jax.shard_map(
        body,
        mesh=mesh,
        in_specs=placed,
        out_specs=(P(("dp", "mp"), None), P(("dp", "mp"))),
        check_vma=False,
    )
```
